128 devices in a mesh: feat: 16 (over x, y_lo, core), batch: 8 (over z, y_hi).
Axes of the slice: x: 4, y: 4 (y_hi: 2, y_lo: 2; y = y_hi * 2 + y_lo), z: 4, core: 2. Of those that a mesh axis runs over, the one named last changes fastest.
Arguments:
- embeddings: bfloat16 [8192, 8192], P('batch', 'feat'), may hold values from -6 to 6
- basis: bfloat16 [8192, 1024], P('feat'), may hold values from -0.0625 to 0.0625
- cov_prior: float32 [8192, 8192], P('feat', 'batch'), may hold values from -1 to 2, as said below
Outputs:
- covariance: float32 [8192, 8192], P('feat', 'batch')
- projected: bfloat16 [8192, 1024], P(('batch', 'feat'))
The draws below stay inside these ranges and needn't reach their ends.
Inputs may be any that keep to these rules, and one draw needn't show every extreme that they name: `cov_prior`: symmetric.
All inputs are finite; a program needn't handle non-finite values.
Results may differ from the reference program's by a relative error of at most 0.011.
Values may be sent and summed in bfloat16 or wider, within the bound.
No kernel may reach another device: no remote copies, remote signals or barrier semaphores. Data moves between devices by JAX's collectives and lax.ppermute only.
A program may use at most 128 MiB of HBM per device.

```python
import math
import jax
import jax.numpy as jnp

D = 8192
K = 1024
ITEMS = 8192


def draw_cov_prior(key, part):
    key = jax.random.fold_in(key, 11)
    key_entries, key_scales = jax.random.split(key)
    entries = jax.random.normal(key_entries, (D, D), jnp.float32)
    mirrored = jnp.clip((entries + entries.T) * 0.7071, -4.0, 4.0)
    scales = jnp.exp(jax.random.uniform(key_scales, (D,), jnp.float32, math.log(0.5), math.log(2.0)))
    root_scale = jnp.sqrt(scales)
    off_terms = mirrored * (root_scale[:, None] * root_scale[None, :]) * (1.0 / math.sqrt(ITEMS))
    positions = jnp.arange(D)
    on_diagonal = positions[:, None] == positions[None, :]
    return jnp.where(on_diagonal, scales[:, None], off_terms).astype(jnp.float32)


def level_of(rng, dims, shards, least, top_value):
    def one(axis_at, shards_of):
        draws = jax.random.uniform(jax.random.fold_in(jax.random.fold_in(rng, 6), axis_at), (shards_of,), jnp.float32, least / len(shards), top_value / len(shards))
        return jnp.repeat(jnp.exp(draws), dims[axis_at] // shards_of).reshape((-1,) + (1,) * (len(dims) - axis_at - 1))

    gain = one(*shards[0])
    for cut in shards[1:]:
        gain = gain * one(*cut)
    return gain


def scatter_about(key, shape, width, limit, shards=(), kind=jnp.bfloat16):
    values = width * jax.random.normal(key, shape, jnp.float32)
    if shards:
        values = values * level_of(key, shape, shards, -0.22, 0.18)
    return jnp.clip(values, -limit, limit).astype(kind)


def setup_inputs(seed: int = 0) -> dict:
    streams_of = jax.random.split(jax.random.key(seed), 4)
    embeddings = scatter_about(streams_of[0], (ITEMS, D), 1.0, 6.0, ((0, 8), (1, 16)))
    basis = scatter_about(streams_of[1], (D, K), D ** -0.5, 0.0625, ((0, 16),))
    cov_prior = draw_cov_prior(jax.random.fold_in(streams_of[3], 71), 0)
    return {"embeddings": embeddings, "basis": basis, "cov_prior": cov_prior}


def reference(embeddings, basis, cov_prior):
    gram = jnp.dot(embeddings.T, embeddings, preferred_element_type=jnp.float32)
    covariance = 0.9 * cov_prior + gram / ITEMS
    projected = jnp.dot(embeddings, basis, preferred_element_type=jnp.float32).astype(jnp.bfloat16)
    return covariance, projected
```

```python
import jax
import jax.numpy as jnp
from jax import lax
from jax.sharding import PartitionSpec as P

CHUNKS = 2
SIZES = (4, 2, 2, 4, 2)
AXES = ("feat", "batch")


def flat(place):
    index = 0
    for value, size in zip(place, SIZES):
        index = index * size + value % size
    return index


def table(move):
    pairs = []
    for x in range(4):
        for yl in range(2):
            for c in range(2):
                for z in range(4):
                    for yh in range(2):
                        pairs.append((flat((x, yl, c, z, yh)), flat(move(x, yl, c, z, yh))))
    return pairs


CORE = table(lambda x, yl, c, z, yh: (x, yl, 1 - c, z, yh))
NEAR = table(lambda x, yl, c, z, yh: (x, 1 - yl, c, z, yh))
FAR = table(lambda x, yl, c, z, yh: (x, 1 - yl, c, z, 1 - yh))
X_STEP = {d: table(lambda x, yl, c, z, yh, d=d: (x + d, yl, c, z, yh)) for d in (1, 2, 3)}
Z_STEP = {d: table(lambda x, yl, c, z, yh, d=d: (x, yl, c, z + d, yh)) for d in (1, 3)}
HOME = {
    (s, t): table(lambda x, yl, c, z, yh, s=s, t=t: (x, yh ^ s, c ^ t, z, 1 - yl))
    for s in range(2)
    for t in range(2)
}


def send(value, pairs):
    return lax.ppermute(value, AXES, pairs)


def columns(array, start, size):
    return lax.dynamic_slice_in_dim(array, start, size, 1)


def pick(array, index):
    return lax.dynamic_index_in_dim(array, index, 0, keepdims=False)


def project(embeddings, basis, x, yl, c):
    total = jnp.dot(embeddings, basis, preferred_element_type=jnp.float32)
    rows, width = total.shape[0] // 16, total.shape[1]
    total = total.reshape(4, 2, 2, rows, width)
    by_core = jnp.moveaxis(total, 2, 0)
    total = pick(by_core, c) + send(
        pick(by_core, 1 - c).astype(jnp.bfloat16), CORE
    ).astype(jnp.float32)
    outgoing = total.astype(jnp.bfloat16)
    mine = pick(total, x)
    for d in (1, 3, 2):
        mine = mine + send(pick(outgoing, (x + d) % 4), X_STEP[d]).astype(jnp.float32)
    mine = pick(mine, yl) + send(pick(mine, 1 - yl).astype(jnp.bfloat16), NEAR).astype(jnp.float32)
    return mine.astype(jnp.bfloat16)


def on_device(embeddings, basis, cov_prior):
    feat, batch = lax.axis_index("feat"), lax.axis_index("batch")
    x, yl, c = feat // 4, feat // 2 % 2, feat % 2
    z, yh = batch // 2, batch % 2
    items, feats = embeddings.shape
    half = feats // 2
    part = half // CHUNKS
    items_total = items * lax.axis_size("batch")

    own = [columns(embeddings, (yh ^ i) * half, half) for i in range(2)]
    near0, far0 = send(own[0], NEAR), send(own[1], FAR)
    right = jnp.concatenate([near0, far0], 0)

    pieces = []
    for k in range(CHUNKS):
        base = right[:, k * part : (k + 1) * part]
        below, above = send(base, X_STEP[1]), send(base, X_STEP[3])
        across = jnp.concatenate(
            [send(below[:items], X_STEP[1]), send(above[items:], X_STEP[3])], 0
        )
        pieces.append(jnp.concatenate([base, above, across, below], 1))

    two0, two1 = send(far0, NEAR), send(near0, FAR)
    near1, far1 = send(own[1], NEAR), send(own[0], FAR)
    groups = [
        jnp.concatenate([own[0], two0], 0),
        jnp.concatenate([own[1], two1], 0),
        right,
        jnp.concatenate([near1, far1], 0),
    ]
    left = jnp.concatenate([g for group in groups for g in (group, send(group, CORE))], 1)

    projected = project(embeddings, basis, x, yl, c)

    arrived = {}
    for k in range(CHUNKS):
        partial = lax.dot_general(
            left, pieces[k], (((0,), (0,)), ((), ())), preferred_element_type=jnp.float32
        ).astype(jnp.bfloat16)
        rows = partial.shape[0] // 2
        block = {d: columns(partial, (z + d - x) % 4 * part, part) for d in range(4)}
        down = send(jnp.stack([block[2][:rows], block[3][rows:]]), Z_STEP[3])
        up = send(jnp.stack([block[1][:rows], block[2][rows:]]), Z_STEP[1])
        first = send(down[0] + block[3][:rows], Z_STEP[3])
        second = send(up[1] + block[1][rows:], Z_STEP[1])

        def total(*terms):
            return sum(t.astype(jnp.float32) for t in terms).astype(jnp.bfloat16)

        whole = jnp.concatenate(
            [
                total(block[0][:rows], up[0], first),
                total(block[0][rows:], down[1], second),
            ],
            0,
        ).reshape(2, 2, 2, half, part)
        for s in range(2):
            chosen = pick(whole, yl ^ yh ^ s)
            for t in range(2):
                outgoing = jnp.concatenate(
                    [pick(chosen[:, t], yh ^ i) for i in range(2)], 0
                )
                arrived[s, t, k] = send(outgoing, HOME[s, t])

    stacked = jnp.stack(
        [
            jnp.concatenate([arrived[s, t, k] for k in range(CHUNKS)], 1)
            for t in range(2)
            for s in range(2)
        ]
    )
    gram = jnp.concatenate(
        [pick(stacked, (q // 2 ^ c) * 2 + (q % 2 ^ yl)) for q in range(4)], 1
    ).astype(jnp.float32)
    covariance = 0.9 * cov_prior + gram / items_total
    return (covariance, projected)


def solution(mesh):
    placed = (P("batch", "feat"), P("feat", None), P("feat", "batch"))
    return jax.shard_map(
        on_device,
        mesh=mesh,
        in_specs=placed,
        out_specs=(P("feat", "batch"), P(("batch", "feat"), None)),
        check_vma=False,
    )
```

```python
import jax
import jax.numpy as jnp
from jax import lax
from jax.sharding import PartitionSpec as P

SIZES = (4, 2, 2, 4, 2)
AXES = ("feat", "batch")


def flat(place):
    index = 0
    for value, size in zip(place, SIZES):
        index = index * size + value % size
    return index


def table(move):
    pairs = []
    for x in range(4):
        for yl in range(2):
            for c in range(2):
                for z in range(4):
                    for yh in range(2):
                        pairs.append((flat((x, yl, c, z, yh)), flat(move(x, yl, c, z, yh))))
    return pairs


CORE = table(lambda x, yl, c, z, yh: (x, yl, 1 - c, z, yh))
NEAR = table(lambda x, yl, c, z, yh: (x, 1 - yl, c, z, yh))
FAR = table(lambda x, yl, c, z, yh: (x, 1 - yl, c, z, 1 - yh))
X_STEP = {d: table(lambda x, yl, c, z, yh, d=d: (x + d, yl, c, z, yh)) for d in (1, 2, 3)}
Z_STEP = {d: table(lambda x, yl, c, z, yh, d=d: (x, yl, c, z + d, yh)) for d in (1, 3)}
HOME = {
    (s, t): table(lambda x, yl, c, z, yh, s=s, t=t: (x, yh ^ s, c ^ t, z, 1 - yl))
    for s in range(2)
    for t in range(2)
}


def send(value, pairs):
    return lax.ppermute(value, AXES, pairs)


def columns(array, start, size):
    return lax.dynamic_slice_in_dim(array, start, size, 1)


def pick(array, index):
    return lax.dynamic_index_in_dim(array, index, 0, keepdims=False)


def wide(value):
    return value.astype(jnp.float32)


def narrow(value):
    return value.astype(jnp.bfloat16)


def together(sends, held):
    values, held = lax.optimization_barrier(([value for value, _ in sends], held))
    results = [send(value, pairs) for value, (_, pairs) in zip(values, sends)]
    return lax.optimization_barrier((results, held))


def on_device(embeddings, basis, cov_prior):
    feat, batch = lax.axis_index("feat"), lax.axis_index("batch")
    x, yl, c = feat // 4, feat // 2 % 2, feat % 2
    z, yh = batch // 2, batch % 2
    items, feats = embeddings.shape
    half = feats // 2
    items_total = items * lax.axis_size("batch")

    own = [columns(embeddings, (yh ^ i) * half, half) for i in range(2)]
    (near, far), own = together([(own[0], NEAR), (own[1], FAR)], own)

    share = jnp.dot(embeddings, basis, preferred_element_type=jnp.float32)
    rows, width = share.shape[0] // 16, share.shape[1]
    share = jnp.moveaxis(share.reshape(4, 2, 2, rows, width), 2, 0)
    share_mine, share_sent = pick(share, c), narrow(pick(share, 1 - c))

    right = jnp.concatenate([near, far], 0)
    (below, above, to_near, to_far, share_got), (right, own, share_mine) = together(
        [
            (right, X_STEP[1]),
            (right, X_STEP[3]),
            (jnp.concatenate([own[1], far], 1), NEAR),
            (jnp.concatenate([own[0], near], 1), FAR),
            (share_sent, CORE),
        ],
        (right, own, share_mine),
    )
    groups = [
        jnp.concatenate([own[0], to_near[:, half:]], 0),
        jnp.concatenate([own[1], to_far[:, half:]], 0),
        right,
        jnp.concatenate([to_near[:, :half], to_far[:, :half]], 0),
    ]
    group = jnp.concatenate(groups, 1)
    share = share_mine + wide(share_got)
    (up_half, down_half, other), (right, above, below, group, share) = together(
        [(below[:items], X_STEP[1]), (above[items:], X_STEP[3]), (group, CORE)],
        (right, above, below, group, share),
    )
    across = jnp.concatenate([up_half, down_half], 0)
    blocks = jnp.stack([right, above, across, below])
    rhs = jnp.concatenate([pick(blocks, (z + d - x) % 4) for d in range(4)], 1)
    partial = [
        narrow(
            lax.dot_general(lhs, rhs, (((0,), (0,)), ((), ())), preferred_element_type=jnp.float32)
        )
        for lhs in (group, other)
    ]
    block = [[p[:, d * half : (d + 1) * half] for p in partial] for d in range(4)]
    outgoing = narrow(share)
    (down, up, *shares), (block, share) = together(
        [
            (jnp.stack([block[2][0], block[3][1]]), Z_STEP[3]),
            (jnp.stack([block[1][0], block[2][1]]), Z_STEP[1]),
        ]
        + [(pick(outgoing, (x + d) % 4), X_STEP[d]) for d in (1, 2, 3)],
        (block, share),
    )
    share = pick(share, x) + sum(wide(s) for s in shares)
    (first, second, share_got), (block, up, down, share) = together(
        [
            (narrow(wide(down[0]) + wide(block[3][0])), Z_STEP[3]),
            (narrow(wide(up[1]) + wide(block[1][1])), Z_STEP[1]),
            (narrow(pick(share, 1 - yl)), NEAR),
        ],
        (block, up, down, share),
    )
    projected = narrow(pick(share, yl) + wide(share_got))
    whole = jnp.stack(
        [
            narrow(wide(block[0][0]) + wide(up[0]) + wide(first)),
            narrow(wide(block[0][1]) + wide(down[1]) + wide(second)),
        ]
    ).reshape(2, 2, 2, half, half)
    homeward = []
    for s in range(2):
        for t in range(2):
            chosen = pick(whole[t], yl ^ yh ^ s)
            value = jnp.concatenate([pick(chosen, yh ^ i) for i in range(2)], 0)
            homeward.append((value, HOME[s, t]))
    arrived, projected = together(homeward, projected)
    arrived = jnp.stack(arrived)
    gram = jnp.concatenate(
        [pick(arrived, (q % 2 ^ yl) * 2 + (q // 2 ^ c)) for q in range(4)], 1
    )
    covariance = 0.9 * cov_prior + wide(gram) / items_total
    return (covariance, projected)


def solution(mesh):
    placed = (P("batch", "feat"), P("feat", None), P("feat", "batch"))
    return jax.shard_map(
        on_device,
        mesh=mesh,
        in_specs=placed,
        out_specs=(P("feat", "batch"), P(("batch", "feat"), None)),
        check_vma=False,
    )
```

```python
import jax
import jax.numpy as jnp
from jax import lax
from jax.experimental import pallas as pl
from jax.experimental.pallas import tpu as pltpu
from jax.sharding import PartitionSpec as P

SIZES = (4, 2, 2, 4, 2)
AXES = ("feat", "batch")


def flat(place):
    index = 0
    for value, size in zip(place, SIZES):
        index = index * size + value % size
    return index


def table(move):
    pairs = []
    for x in range(4):
        for yl in range(2):
            for c in range(2):
                for z in range(4):
                    for yh in range(2):
                        pairs.append((flat((x, yl, c, z, yh)), flat(move(x, yl, c, z, yh))))
    return pairs


CORE = table(lambda x, yl, c, z, yh: (x, yl, 1 - c, z, yh))
NEAR = table(lambda x, yl, c, z, yh: (x, 1 - yl, c, z, yh))
FAR = table(lambda x, yl, c, z, yh: (x, 1 - yl, c, z, 1 - yh))
X_STEP = {d: table(lambda x, yl, c, z, yh, d=d: (x + d, yl, c, z, yh)) for d in (1, 2, 3)}
Z_STEP = {d: table(lambda x, yl, c, z, yh, d=d: (x, yl, c, z + d, yh)) for d in (1, 3)}
HOME = {
    (s, t): table(lambda x, yl, c, z, yh, s=s, t=t: (x, yh ^ s, c ^ t, z, 1 - yl))
    for s in range(2)
    for t in range(2)
}


def send(value, pairs):
    return lax.ppermute(value, AXES, pairs)


def pick(array, index):
    return lax.dynamic_index_in_dim(array, index, 0, keepdims=False)


def wide(value):
    return value.astype(jnp.float32)


def narrow(value):
    return value.astype(jnp.bfloat16)


def together(sends, held):
    values, held = lax.optimization_barrier(([value for value, _ in sends], held))
    results = [send(value, pairs) for value, (_, pairs) in zip(values, sends)]
    return lax.optimization_barrier((results, held))


def block_kernel(
    shift_ref,
    own, right, to_near, to_far,
    own_c, right_c, to_near_c, to_far_c,
    above, below, across_up, across_down,
    down, up, middle, home,
    left, columns_in, result, left_sem, column_sem, out_sem,
):
    shift = shift_ref[0]
    rights = []
    sources = ((right, 0), (above, 1), (below, 3), (across_up, 2), (across_down, 2))
    for n, (source, dx) in enumerate(sources):
        dz = (shift + dx) % 4
        target = columns_in.at[dz] if n < 3 else columns_in.at[dz, n - 3]
        rights.append(pltpu.make_async_copy(source, target, column_sem.at[n]))
    lefts = [
        pltpu.make_async_copy(source, left.at[n // 4, n % 4], left_sem.at[n])
        for n, source in enumerate(
            (own, right, to_near, to_far, own_c, right_c, to_near_c, to_far_c)
        )
    ]
    for copy in lefts[:4] + rights + lefts[4:]:
        copy.start()
    for copy in lefts[:4] + rights:
        copy.wait()
    rows = own.shape[1]

    def multiply(cc):
        pairs = (((0, 0), (2, 1)), ((0, 1), (3, 1)), ((1, 0), (1, 1)), ((2, 0), (3, 0)))

        def step(dz, carry):
            for g, pair in enumerate(pairs):
                total = None
                for i, (piece, half) in enumerate(pair):
                    term = lax.dot_general(
                        left[cc, piece, half],
                        columns_in[dz, i],
                        (((1,), (1,)), ((), ())),
                        preferred_element_type=jnp.float32,
                    )
                    total = term if total is None else total + term
                result[cc, dz, g * rows : (g + 1) * rows, :] = total.astype(jnp.bfloat16)
            return carry

        lax.fori_loop(0, 4, step, 0)

    outs = []
    for cc, targets in enumerate(((home, up, down, middle), (home, middle, up, down))):
        if cc:
            for copy in lefts[4:]:
                copy.wait()
        multiply(cc)
        for dz, target in enumerate(targets):
            copy = pltpu.make_async_copy(
                result.at[cc, dz], target.at[cc], out_sem.at[cc * 4 + dz]
            )
            copy.start()
            outs.append(copy)
    for copy in outs:
        copy.wait()


def block_product(shift, left, left_c, above, below, across_up, across_down):
    _, half, items = left[0].shape
    anywhere = pl.BlockSpec(memory_space=pl.ANY)
    message = jax.ShapeDtypeStruct((2, 4 * half, half), jnp.bfloat16)
    operands = (*left, *left_c, above, below, across_up, across_down)
    return pl.pallas_call(
        block_kernel,
        out_shape=[message] * 4,
        in_specs=[pl.BlockSpec(memory_space=pltpu.SMEM)] + [anywhere] * len(operands),
        out_specs=[anywhere] * 4,
        scratch_shapes=[
            pltpu.VMEM((2, 4, 2, half, items), jnp.bfloat16),
            pltpu.VMEM((4, 2, half, items), jnp.bfloat16),
            pltpu.VMEM((2, 4, 4 * half, half), jnp.bfloat16),
            pltpu.SemaphoreType.DMA((8,)),
            pltpu.SemaphoreType.DMA((5,)),
            pltpu.SemaphoreType.DMA((8,)),
        ],
        compiler_params=pltpu.CompilerParams(vmem_limit_bytes=24 * 1024 * 1024),
        cost_estimate=pl.CostEstimate(
            flops=2 * 8 * half * 4 * half * 2 * items,
            bytes_accessed=32 * half * items * 2 + 32 * half * half * 2,
            transcendentals=0,
        ),
    )(shift, *operands)


def on_device(embeddings, basis, cov_prior):
    feat, batch = lax.axis_index("feat"), lax.axis_index("batch")
    x, yl, c = feat // 4, feat // 2 % 2, feat % 2
    z, yh = batch // 2, batch % 2
    items, feats = embeddings.shape
    half = feats // 2
    items_total = items * lax.axis_size("batch")

    halves = embeddings.T.reshape(2, half, items)
    own = jnp.stack([pick(halves, yh), pick(halves, 1 - yh)])
    (near, far, own_c), own = together([(own[0], NEAR), (own[1], FAR), (own, CORE)], own)

    share = jnp.dot(embeddings, basis, preferred_element_type=jnp.float32)
    rows, width = share.shape[0] // 16, share.shape[1]
    share = jnp.moveaxis(share.reshape(4, 2, 2, rows, width), 2, 0)
    share_mine, share_sent = pick(share, c), narrow(pick(share, 1 - c))

    right = jnp.stack([near, far])
    (below, above, to_near, to_far, right_c), (right, own, own_c, share_mine) = together(
        [
            (right, X_STEP[1]),
            (right, X_STEP[3]),
            (jnp.stack([own[1], far]), NEAR),
            (jnp.stack([own[0], near]), FAR),
            (right, CORE),
        ],
        (right, own, own_c, share_mine),
    )
    (across_up, across_down, to_near_c, to_far_c, share_got), held = together(
        [
            (below[0], X_STEP[1]),
            (above[1], X_STEP[3]),
            (to_near, CORE),
            (to_far, CORE),
            (share_sent, CORE),
        ],
        (right, above, below, own, own_c, right_c, to_near, to_far, share_mine),
    )
    right, above, below, own, own_c, right_c, to_near, to_far, share_mine = held
    share = share_mine + wide(share_got)
    down, up, middle, home = block_product(
        ((x - z) % 4).astype(jnp.int32).reshape(1),
        (own, right, to_near, to_far),
        (own_c, right_c, to_near_c, to_far_c),
        above, below, across_up, across_down,
    )
    outgoing = narrow(share)
    (down, up, *shares), (middle, home, share) = together(
        [(down, Z_STEP[3]), (up, Z_STEP[1])]
        + [(pick(outgoing, (x + d) % 4), X_STEP[d]) for d in (1, 2, 3)],
        (middle, home, share),
    )
    share = pick(share, x) + sum(wide(s) for s in shares)
    (first, second, share_got), (home, up, down, share) = together(
        [
            (narrow(wide(down[0]) + wide(middle[0])), Z_STEP[3]),
            (narrow(wide(up[1]) + wide(middle[1])), Z_STEP[1]),
            (narrow(pick(share, 1 - yl)), NEAR),
        ],
        (home, up, down, share),
    )
    projected = narrow(pick(share, yl) + wide(share_got))
    whole = [
        narrow(wide(home[0]) + wide(up[0]) + wide(first)).reshape(2, 2, half, half),
        narrow(wide(home[1]) + wide(down[1]) + wide(second)).reshape(2, 2, half, half),
    ]
    homeward = []
    for s in range(2):
        for t in range(2):
            chosen = pick(whole[t], yl ^ yh ^ s)
            value = jnp.concatenate([pick(chosen, yh ^ i) for i in range(2)], 0)
            homeward.append((value, HOME[s, t]))
    arrived, projected = together(homeward, projected)
    arrived = jnp.stack(arrived)
    gram = jnp.concatenate(
        [pick(arrived, (q % 2 ^ yl) * 2 + (q // 2 ^ c)) for q in range(4)], 1
    )
    covariance = 0.9 * cov_prior + wide(gram) / items_total
    return (covariance, projected)


def solution(mesh):
    placed = (P("batch", "feat"), P("feat", None), P("feat", "batch"))
    return jax.shard_map(
        on_device,
        mesh=mesh,
        in_specs=placed,
        out_specs=(P("feat", "batch"), P(("batch", "feat"), None)),
        check_vma=False,
    )
```

```python
import functools

import jax
import jax.numpy as jnp
from jax import lax
from jax.experimental import pallas as pl
from jax.experimental.pallas import tpu as pltpu
from jax.sharding import PartitionSpec as P

SIZES = (4, 2, 2, 4, 2)
AXES = ("feat", "batch")


def flat(place):
    index = 0
    for value, size in zip(place, SIZES):
        index = index * size + value % size
    return index


def table(move):
    pairs = []
    for x in range(4):
        for yl in range(2):
            for c in range(2):
                for z in range(4):
                    for yh in range(2):
                        pairs.append((flat((x, yl, c, z, yh)), flat(move(x, yl, c, z, yh))))
    return pairs


CORE = table(lambda x, yl, c, z, yh: (x, yl, 1 - c, z, yh))
NEAR = table(lambda x, yl, c, z, yh: (x, 1 - yl, c, z, yh))
FAR = table(lambda x, yl, c, z, yh: (x, 1 - yl, c, z, 1 - yh))
X_STEP = {d: table(lambda x, yl, c, z, yh, d=d: (x + d, yl, c, z, yh)) for d in (1, 2, 3)}
Z_STEP = {d: table(lambda x, yl, c, z, yh, d=d: (x, yl, c, z + d, yh)) for d in (1, 3)}
HOME = {
    (s, t): table(lambda x, yl, c, z, yh, s=s, t=t: (x, yh ^ s, c ^ t, z, 1 - yl))
    for s in range(2)
    for t in range(2)
}


def send(value, pairs):
    return lax.ppermute(value, AXES, pairs)


def pick(array, index):
    return lax.dynamic_index_in_dim(array, index, 0, keepdims=False)


def wide(value):
    return value.astype(jnp.float32)


def narrow(value):
    return value.astype(jnp.bfloat16)


def together(sends, after=()):
    values, _ = lax.optimization_barrier(([value for value, _ in sends], after))
    results = [send(value, pairs) for value, (_, pairs) in zip(values, sends)]
    return lax.optimization_barrier(results)


def block_kernel(plan, sides, offsets, *refs):
    place, refs = refs[0], refs[1:]
    n_in = plan["inputs"]
    inputs, refs = refs[:n_in], refs[n_in + plan["kept"] :]
    targets, refs = refs[: plan["targets"]], refs[plan["targets"] :]
    left, columns_in, result, left_sem, column_sem, out_sem = refs
    shift, high = place[0], place[1]

    def view(name):
        index, part = name
        if part is None:
            return inputs[index]
        return inputs[index].at[part if isinstance(part, int) else (high ^ int(part))]

    rights = [
        pltpu.make_async_copy(view(name), columns_in.at[n, i], column_sem.at[2 * n + i])
        for n, names in enumerate(plan["blocks"])
        for i, name in enumerate(names)
    ]
    lefts = [
        pltpu.make_async_copy(view(name), left.at[k, i], left_sem.at[2 * k + i])
        for k, names in enumerate(sides)
        for i, name in enumerate(names)
    ]
    for copy in rights[:2] + lefts[:2] + rights[2:] + lefts[2:]:
        copy.start()
    for copy in rights:
        copy.wait()
    rows = columns_in.shape[2]
    outs = []
    for k in range(len(sides)):
        for copy in lefts[2 * k : 2 * k + 2]:
            copy.wait()
        side, group = divmod(k, 4)
        for n in range(len(offsets)):
            total = None
            for i in range(2):
                term = lax.dot_general(
                    left[k, i],
                    columns_in[n, i],
                    (((1,), (1,)), ((), ())),
                    preferred_element_type=jnp.float32,
                )
                total = term if total is None else total + term
            result[side, n, group * rows : (group + 1) * rows, :] = total.astype(jnp.bfloat16)
        if group == 3:
            for n, dx in enumerate(offsets):
                dz = (shift + dx) % 4
                for d in range(4):
                    copy = pltpu.make_async_copy(
                        result.at[side, n],
                        targets[side * 4 + d],
                        out_sem.at[side * len(offsets) + n],
                    )
                    outs.append((dz == d, copy))
                    pl.when(dz == d)(copy.start)
    for here, copy in outs:
        pl.when(here)(copy.wait)


def block_product(place, sides, blocks, kept=()):
    inputs = []

    def enter(piece):
        array, part = piece if isinstance(piece, tuple) else (piece, None)
        for index, known in enumerate(inputs):
            if known is array:
                return index, part
        inputs.append(array)
        return len(inputs) - 1, part

    groups = [[enter(piece) for piece in pair] for side in sides for pair in side]
    names = [[enter(piece) for piece in pair] for pair in blocks.values()]
    half, items = inputs[0].shape[-2:]
    n_targets = 4 * len(sides)
    plan = {"inputs": len(inputs), "kept": len(kept), "targets": n_targets, "blocks": names}
    anywhere = pl.BlockSpec(memory_space=pl.ANY)
    n_blocks = len(blocks)
    return pl.pallas_call(
        functools.partial(block_kernel, plan, groups, tuple(blocks)),
        out_shape=[jax.ShapeDtypeStruct((4 * half, half), jnp.bfloat16)] * n_targets,
        in_specs=[pl.BlockSpec(memory_space=pltpu.SMEM)]
        + [anywhere] * (len(inputs) + len(kept)),
        out_specs=[anywhere] * n_targets,
        input_output_aliases={1 + len(inputs) + n: n for n in range(len(kept))},
        scratch_shapes=[
            pltpu.VMEM((len(groups), 2, half, items), jnp.bfloat16),
            pltpu.VMEM((n_blocks, 2, half, items), jnp.bfloat16),
            pltpu.VMEM((len(sides), n_blocks, 4 * half, half), jnp.bfloat16),
            pltpu.SemaphoreType.DMA((2 * len(groups),)),
            pltpu.SemaphoreType.DMA((2 * n_blocks,)),
            pltpu.SemaphoreType.DMA((len(sides) * n_blocks,)),
        ],
        compiler_params=pltpu.CompilerParams(vmem_limit_bytes=20 * 1024 * 1024),
        cost_estimate=pl.CostEstimate(
            flops=2 * len(sides) * 4 * half * n_blocks * half * 2 * items,
            bytes_accessed=(len(groups) + n_blocks) * 4 * half * items,
            transcendentals=0,
        ),
    )(place, *inputs, *kept)


def on_device(embeddings, basis, cov_prior):
    feat, batch = lax.axis_index("feat"), lax.axis_index("batch")
    x, yl, c = feat // 4, feat // 2 % 2, feat % 2
    z, yh = batch // 2, batch % 2
    items, feats = embeddings.shape
    half = feats // 2
    items_total = items * lax.axis_size("batch")
    place = jnp.stack([(x - z) % 4, yh]).astype(jnp.int32)

    whole = embeddings.T.reshape(2, half, items)
    inner, outer = pick(whole, yh), pick(whole, 1 - yh)
    near, far = together([(inner, NEAR), (outer, FAR)])
    right = jnp.stack([near, far])

    below_n, above_f, near1, far1, whole_c = together(
        [(near, X_STEP[1]), (far, X_STEP[3]), (outer, NEAR), (inner, FAR), (whole, CORE)]
    )
    share = jnp.dot(embeddings, basis, preferred_element_type=jnp.float32)
    rows, width = share.shape[0] // 16, share.shape[1]
    share = jnp.moveaxis(share.reshape(4, 2, 2, rows, width), 2, 0)
    share_sent = narrow(pick(share, 1 - c))
    rim = jnp.stack([near1, far1])

    below_f, above_n, two0, two1, right_c = together(
        [(far, X_STEP[1]), (near, X_STEP[3]), (far, NEAR), (near, FAR), (right, CORE)],
        (below_n, above_f),
    )
    two = jnp.stack([two0, two1])
    rim_c, two_c = together([(rim, CORE), (two, CORE)], (below_f, above_n))
    across = together([(below_n, X_STEP[1]), (above_f, X_STEP[3])], (below_f, above_n))
    (share_got,) = together([(share_sent, CORE)], (below_f, above_n))
    side = (
        ((whole, "0"), two0),
        ((whole, "1"), two1),
        (near, far),
        (near1, far1),
    )
    side_c = (
        ((whole_c, "0"), (two_c, 0)),
        ((whole_c, "1"), (two_c, 1)),
        ((right_c, 0), (right_c, 1)),
        ((rim_c, 0), (rim_c, 1)),
    )
    early = {0: (near, far), 1: (above_n, above_f), 3: (below_n, below_f)}
    a = block_product(place, [side], early)
    b = block_product(place, [side_c], early)
    across, a, b = lax.optimization_barrier((across, a, b))
    a0, a1, a2, a3, b0, b1, b2, b3 = block_product(
        place, [side, side_c], {2: tuple(across)}, (*a, *b)
    )

    down_a, up_b, down_b, up_a = together(
        [(a2, Z_STEP[3]), (b2, Z_STEP[1]), (b3, Z_STEP[3]), (a1, Z_STEP[1])]
    )
    share = pick(share, c) + wide(share_got)
    outgoing = narrow(share)
    first, second, *shares = together(
        [(narrow(wide(down_a) + wide(a3)), Z_STEP[3]), (narrow(wide(up_b) + wide(b1)), Z_STEP[1])]
        + [(pick(outgoing, (x + d) % 4), X_STEP[d]) for d in (1, 3, 2)]
    )
    share = pick(share, x) + sum(wide(s) for s in shares)
    total = [
        narrow(wide(a0) + wide(up_a) + wide(first)).reshape(2, 2, half, half),
        narrow(wide(b0) + wide(down_b) + wide(second)).reshape(2, 2, half, half),
    ]
    homeward = []
    for s in range(2):
        for t in range(2):
            chosen = pick(total[t], yl ^ yh ^ s)
            value = jnp.concatenate([pick(chosen, yh ^ i) for i in range(2)], 0)
            homeward.append((value, HOME[s, t]))
    *arrived, share_got = together(homeward + [(narrow(pick(share, 1 - yl)), NEAR)])
    projected = narrow(pick(share, yl) + wide(share_got))
    arrived = jnp.stack(arrived)
    gram = jnp.concatenate(
        [pick(arrived, (q % 2 ^ yl) * 2 + (q // 2 ^ c)) for q in range(4)], 1
    )
    covariance = 0.9 * cov_prior + wide(gram) / items_total
    return (covariance, projected)


def solution(mesh):
    placed = (P("batch", "feat"), P("feat", None), P("feat", "batch"))
    return jax.shard_map(
        on_device,
        mesh=mesh,
        in_specs=placed,
        out_specs=(P("feat", "batch"), P(("batch", "feat"), None)),
        check_vma=False,
    )
```

```python
import functools

import jax
import jax.numpy as jnp
from jax import lax
from jax.experimental import pallas as pl
from jax.experimental.pallas import tpu as pltpu
from jax.sharding import PartitionSpec as P

SIZES = (4, 2, 2, 4, 2)
AXES = ("feat", "batch")


def flat(place):
    index = 0
    for value, size in zip(place, SIZES):
        index = index * size + value % size
    return index


def table(move):
    pairs = []
    for x in range(4):
        for yl in range(2):
            for c in range(2):
                for z in range(4):
                    for yh in range(2):
                        pairs.append((flat((x, yl, c, z, yh)), flat(move(x, yl, c, z, yh))))
    return pairs


CORE = table(lambda x, yl, c, z, yh: (x, yl, 1 - c, z, yh))
NEAR = table(lambda x, yl, c, z, yh: (x, 1 - yl, c, z, yh))
FAR = table(lambda x, yl, c, z, yh: (x, 1 - yl, c, z, 1 - yh))
X_STEP = {d: table(lambda x, yl, c, z, yh, d=d: (x + d, yl, c, z, yh)) for d in (1, 2, 3)}
Z_STEP = {d: table(lambda x, yl, c, z, yh, d=d: (x, yl, c, z + d, yh)) for d in (1, 3)}
HOME = {
    (s, t): table(lambda x, yl, c, z, yh, s=s, t=t: (x, yh ^ s, c ^ t, z, 1 - yl))
    for s in range(2)
    for t in range(2)
}


def send(value, pairs):
    return lax.ppermute(value, AXES, pairs)


def pick(array, index):
    return lax.dynamic_index_in_dim(array, index, 0, keepdims=False)


def wide(value):
    return value.astype(jnp.float32)


def narrow(value):
    return value.astype(jnp.bfloat16)


def together(sends, after=()):
    values, _ = lax.optimization_barrier(([value for value, _ in sends], after))
    results = [send(value, pairs) for value, (_, pairs) in zip(values, sends)]
    return lax.optimization_barrier(results)


def block_kernel(plan, sides, offsets, *refs):
    place, refs = refs[0], refs[1:]
    n_in = plan["inputs"]
    inputs, refs = refs[:n_in], refs[n_in + plan["kept"] :]
    home, up, down, middle = refs[:4]
    targets, refs = ((home, up, down, middle), (home, middle, up, down)), refs[4:]
    left, columns_in, result, left_sem, column_sem, out_sem = refs
    shift, high = place[0], place[1]

    def view(name):
        index, part = name
        if part is None:
            return inputs[index]
        return inputs[index].at[part if isinstance(part, int) else (high ^ int(part))]

    rights = [
        pltpu.make_async_copy(view(name), columns_in.at[n, i], column_sem.at[2 * n + i])
        for n, names in enumerate(plan["blocks"])
        for i, name in enumerate(names)
    ]
    lefts = [
        pltpu.make_async_copy(view(name), left.at[k, i], left_sem.at[2 * k + i])
        for k, names in enumerate(sides)
        for i, name in enumerate(names)
    ]
    for copy in rights[:2] + lefts[:2] + rights[2:] + lefts[2:]:
        copy.start()
    for copy in rights:
        copy.wait()
    rows = columns_in.shape[2]
    outs = []
    for k in range(len(sides)):
        for copy in lefts[2 * k : 2 * k + 2]:
            copy.wait()
        side, group = divmod(k, 4)
        for n in range(len(offsets)):
            total = None
            for i in range(2):
                term = lax.dot_general(
                    left[k, i],
                    columns_in[n, i],
                    (((1,), (1,)), ((), ())),
                    preferred_element_type=jnp.float32,
                )
                total = term if total is None else total + term
            result[side, n, group * rows : (group + 1) * rows, :] = total.astype(jnp.bfloat16)
        if group == 3:
            for n, dx in enumerate(offsets):
                dz = (shift + dx) % 4
                for d in range(4):
                    cc = plan["sides"][side]
                    copy = pltpu.make_async_copy(
                        result.at[side, n],
                        targets[cc][d].at[cc],
                        out_sem.at[side * len(offsets) + n],
                    )
                    outs.append((dz == d, copy))
                    pl.when(dz == d)(copy.start)
    for here, copy in outs:
        pl.when(here)(copy.wait)


def block_product(place, sides, blocks, kept=()):
    inputs = []

    def enter(piece):
        array, part = piece if isinstance(piece, tuple) else (piece, None)
        for index, known in enumerate(inputs):
            if known is array:
                return index, part
        inputs.append(array)
        return len(inputs) - 1, part

    groups = [[enter(piece) for piece in pair] for side in sides.values() for pair in side]
    names = [[enter(piece) for piece in pair] for pair in blocks.values()]
    half, items = inputs[0].shape[-2:]
    plan = {"inputs": len(inputs), "kept": len(kept), "sides": tuple(sides), "blocks": names}
    outside = pl.BlockSpec(memory_space=pltpu.HBM)
    n_blocks = len(blocks)
    return pl.pallas_call(
        functools.partial(block_kernel, plan, groups, tuple(blocks)),
        out_shape=[jax.ShapeDtypeStruct((2, 4 * half, half), jnp.bfloat16)] * 4,
        in_specs=[pl.BlockSpec(memory_space=pltpu.SMEM)]
        + [outside] * (len(inputs) + len(kept)),
        out_specs=[outside] * 4,
        input_output_aliases={1 + len(inputs) + n: n for n in range(len(kept))},
        scratch_shapes=[
            pltpu.VMEM((len(groups), 2, half, items), jnp.bfloat16),
            pltpu.VMEM((n_blocks, 2, half, items), jnp.bfloat16),
            pltpu.VMEM((len(sides), n_blocks, 4 * half, half), jnp.bfloat16),
            pltpu.SemaphoreType.DMA((2 * len(groups),)),
            pltpu.SemaphoreType.DMA((2 * n_blocks,)),
            pltpu.SemaphoreType.DMA((len(sides) * n_blocks,)),
        ],
        compiler_params=pltpu.CompilerParams(vmem_limit_bytes=60 * 1024 * 1024),
        cost_estimate=pl.CostEstimate(
            flops=half * half, bytes_accessed=half * items, transcendentals=0
        ),
    )(place, *inputs, *kept)


def on_device(embeddings, basis, cov_prior):
    feat, batch = lax.axis_index("feat"), lax.axis_index("batch")
    x, yl, c = feat // 4, feat // 2 % 2, feat % 2
    z, yh = batch // 2, batch % 2
    items, feats = embeddings.shape
    half = feats // 2
    items_total = items * lax.axis_size("batch")
    place = jnp.stack([(x - z) % 4, yh]).astype(jnp.int32)

    whole = embeddings.T.reshape(2, half, items)
    inner, outer = pick(whole, yh), pick(whole, 1 - yh)
    near, far, whole_c = together([(inner, NEAR), (outer, FAR), (whole, CORE)])
    right = jnp.stack([near, far])
    share = jnp.dot(embeddings, basis, preferred_element_type=jnp.float32)
    rows, width = share.shape[0] // 16, share.shape[1]
    share = jnp.moveaxis(share.reshape(4, 2, 2, rows, width), 2, 0)
    share_sent = narrow(pick(share, 1 - c))

    below_n, above_f, near1, far1, share_got = together(
        [
            (near, X_STEP[1]),
            (far, X_STEP[3]),
            (outer, NEAR),
            (inner, FAR),
            (share_sent, CORE),
        ]
    )
    below_f, above_n, two0, two1, right_c = together(
        [(far, X_STEP[1]), (near, X_STEP[3]), (far, NEAR), (near, FAR), (right, CORE)],
        (below_n, above_f),
    )
    rim = jnp.stack([near1, far1])
    share = pick(share, c) + wide(share_got)
    outgoing = narrow(share)
    rim_c, two0_c, two1_c = together(
        [(rim, CORE), (two0, CORE), (two1, CORE)], (below_f, above_n)
    )
    across = together([(below_n, X_STEP[1]), (above_f, X_STEP[3])], (below_f, above_n))
    side = (
        ((whole, "0"), two0),
        ((whole, "1"), two1),
        (near, far),
        (near1, far1),
    )
    side_c = (
        ((whole_c, "0"), two0_c),
        ((whole_c, "1"), two1_c),
        ((right_c, 0), (right_c, 1)),
        ((rim_c, 0), (rim_c, 1)),
    )
    early = {0: (near, far), 1: (above_n, above_f), 3: (below_n, below_f)}
    kept = block_product(place, {0: side}, early)
    kept = block_product(place, {1: side_c}, early, kept)
    across, kept = lax.optimization_barrier((across, kept))
    home, up, down, middle = block_product(
        place, {0: side, 1: side_c}, {2: tuple(across)}, kept
    )

    down, up, *shares = together(
        [(down, Z_STEP[3]), (up, Z_STEP[1])]
        + [(pick(outgoing, (x + d) % 4), X_STEP[d]) for d in (1, 2, 3)]
    )
    first, second = together(
        [
            (narrow(wide(down[0]) + wide(middle[0])), Z_STEP[3]),
            (narrow(wide(up[1]) + wide(middle[1])), Z_STEP[1]),
        ]
    )
    share = pick(share, x) + sum(wide(s) for s in shares)
    total = [
        narrow(wide(home[0]) + wide(up[0]) + wide(first)).reshape(2, 2, half, half),
        narrow(wide(home[1]) + wide(down[1]) + wide(second)).reshape(2, 2, half, half),
    ]
    homeward = []
    for s in range(2):
        for t in range(2):
            chosen = pick(total[t], yl ^ yh ^ s)
            value = jnp.concatenate([pick(chosen, yh ^ i) for i in range(2)], 0)
            homeward.append((value, HOME[s, t]))
    *arrived, share_got = together(homeward + [(narrow(pick(share, 1 - yl)), NEAR)])
    projected = narrow(pick(share, yl) + wide(share_got))
    arrived = jnp.stack(arrived)
    gram = jnp.concatenate(
        [pick(arrived, (q % 2 ^ yl) * 2 + (q // 2 ^ c)) for q in range(4)], 1
    )
    covariance = 0.9 * cov_prior + wide(gram) / items_total
    return (covariance, projected)


def solution(mesh):
    placed = (P("batch", "feat"), P("feat", None), P("feat", "batch"))
    return jax.shard_map(
        on_device,
        mesh=mesh,
        in_specs=placed,
        out_specs=(P("feat", "batch"), P(("batch", "feat"), None)),
        check_vma=False,
    )
```

```python
import functools

import jax
import jax.numpy as jnp
from jax import lax
from jax.experimental import pallas as pl
from jax.experimental.pallas import tpu as pltpu
from jax.sharding import PartitionSpec as P

SIZES = (4, 2, 2, 4, 2)
AXES = ("feat", "batch")


def flat(place):
    index = 0
    for value, size in zip(place, SIZES):
        index = index * size + value % size
    return index


def table(move):
    pairs = []
    for x in range(4):
        for yl in range(2):
            for c in range(2):
                for z in range(4):
                    for yh in range(2):
                        pairs.append((flat((x, yl, c, z, yh)), flat(move(x, yl, c, z, yh))))
    return pairs


CORE = table(lambda x, yl, c, z, yh: (x, yl, 1 - c, z, yh))
NEAR = table(lambda x, yl, c, z, yh: (x, 1 - yl, c, z, yh))
FAR = table(lambda x, yl, c, z, yh: (x, 1 - yl, c, z, 1 - yh))
X_STEP = {d: table(lambda x, yl, c, z, yh, d=d: (x + d, yl, c, z, yh)) for d in (1, 2, 3)}
Z_STEP = {d: table(lambda x, yl, c, z, yh, d=d: (x, yl, c, z + d, yh)) for d in (1, 3)}
HOME = {
    (s, t): table(lambda x, yl, c, z, yh, s=s, t=t: (x, yh ^ s, c ^ t, z, 1 - yl))
    for s in range(2)
    for t in range(2)
}


def send(value, pairs):
    return lax.ppermute(value, AXES, pairs)


def pick(array, index):
    return lax.dynamic_index_in_dim(array, index, 0, keepdims=False)


def wide(value):
    return value.astype(jnp.float32)


def narrow(value):
    return value.astype(jnp.bfloat16)


def together(sends, after=()):
    values, _ = lax.optimization_barrier(([value for value, _ in sends], after))
    results = [send(value, pairs) for value, (_, pairs) in zip(values, sends)]
    return lax.optimization_barrier(results)


def block_kernel(plan, sides, offsets, *refs):
    place, refs = refs[0], refs[1:]
    n_in = plan["inputs"]
    inputs, refs = refs[:n_in], refs[n_in + plan["kept"] :]
    home, up, down, middle = refs[:4]
    targets, refs = ((home, up, down, middle), (home, middle, up, down)), refs[4:]
    left, columns_in, result, left_sem, column_sem, out_sem = refs
    shift, high = place[0], place[1]

    def view(name):
        index, part = name
        if part is None:
            return inputs[index]
        return inputs[index].at[part if isinstance(part, int) else (high ^ int(part))]

    rights = [
        pltpu.make_async_copy(view(name), columns_in.at[n, i], column_sem.at[2 * n + i])
        for n, names in enumerate(plan["blocks"])
        for i, name in enumerate(names)
    ]
    lefts = [
        pltpu.make_async_copy(view(name), left.at[k, i], left_sem.at[2 * k + i])
        for k, names in enumerate(sides)
        for i, name in enumerate(names)
    ]
    for copy in rights[:2] + lefts[:2] + rights[2:] + lefts[2:]:
        copy.start()
    for copy in rights:
        copy.wait()
    rows = columns_in.shape[2]
    n_offsets = len(offsets)
    outs = []

    def multiply(step, carry):
        k, n = step // n_offsets, step % n_offsets

        @pl.when(n == 0)
        def _():
            for i in range(2):
                piece = left.at[k, i]
                pltpu.make_async_copy(piece, piece, left_sem.at[2 * k + i]).wait()

        total = sum(
            lax.dot_general(
                left[k, i],
                columns_in[n, i],
                (((1,), (1,)), ((), ())),
                preferred_element_type=jnp.float32,
            )
            for i in range(2)
        )
        place_in = pl.ds(pl.multiple_of(k % 4 * rows, rows), rows)
        result[k // 4, n, place_in, :] = total.astype(jnp.bfloat16)
        return carry

    for side, cc in enumerate(plan["sides"]):
        lax.fori_loop(4 * n_offsets * side, 4 * n_offsets * (side + 1), multiply, 0)
        for n, dx in enumerate(offsets):
            dz = (shift + dx) % 4
            for d in range(4):
                copy = pltpu.make_async_copy(
                    result.at[side, n],
                    targets[cc][d].at[cc],
                    out_sem.at[side * n_offsets + n],
                )
                outs.append((dz == d, copy))
                pl.when(dz == d)(copy.start)
    for here, copy in outs:
        pl.when(here)(copy.wait)


def block_product(place, sides, blocks, kept=()):
    inputs = []

    def enter(piece):
        array, part = piece if isinstance(piece, tuple) else (piece, None)
        for index, known in enumerate(inputs):
            if known is array:
                return index, part
        inputs.append(array)
        return len(inputs) - 1, part

    groups = [[enter(piece) for piece in pair] for side in sides.values() for pair in side]
    names = [[enter(piece) for piece in pair] for pair in blocks.values()]
    half, items = inputs[0].shape[-2:]
    plan = {"inputs": len(inputs), "kept": len(kept), "sides": tuple(sides), "blocks": names}
    outside = pl.BlockSpec(memory_space=pltpu.HBM)
    n_blocks = len(blocks)
    return pl.pallas_call(
        functools.partial(block_kernel, plan, groups, tuple(blocks)),
        out_shape=[jax.ShapeDtypeStruct((2, 4 * half, half), jnp.bfloat16)] * 4,
        in_specs=[pl.BlockSpec(memory_space=pltpu.SMEM)]
        + [outside] * (len(inputs) + len(kept)),
        out_specs=[outside] * 4,
        input_output_aliases={1 + len(inputs) + n: n for n in range(len(kept))},
        scratch_shapes=[
            pltpu.VMEM((len(groups), 2, half, items), jnp.bfloat16),
            pltpu.VMEM((n_blocks, 2, half, items), jnp.bfloat16),
            pltpu.VMEM((len(sides), n_blocks, 4 * half, half), jnp.bfloat16),
            pltpu.SemaphoreType.DMA((2 * len(groups),)),
            pltpu.SemaphoreType.DMA((2 * n_blocks,)),
            pltpu.SemaphoreType.DMA((len(sides) * n_blocks,)),
        ],
        compiler_params=pltpu.CompilerParams(vmem_limit_bytes=60 * 1024 * 1024),
        cost_estimate=pl.CostEstimate(
            flops=half * half, bytes_accessed=half * items, transcendentals=0
        ),
    )(place, *inputs, *kept)


def on_device(embeddings, basis, cov_prior):
    feat, batch = lax.axis_index("feat"), lax.axis_index("batch")
    x, yl, c = feat // 4, feat // 2 % 2, feat % 2
    z, yh = batch // 2, batch % 2
    items, feats = embeddings.shape
    half = feats // 2
    items_total = items * lax.axis_size("batch")
    place = jnp.stack([(x - z) % 4, yh]).astype(jnp.int32)

    whole = embeddings.T.reshape(2, half, items)
    inner, outer = pick(whole, yh), pick(whole, 1 - yh)
    near, far, whole_c = together([(inner, NEAR), (outer, FAR), (whole, CORE)])
    right = jnp.stack([near, far])
    share = narrow(jnp.dot(embeddings, basis, preferred_element_type=jnp.float32))
    width = share.shape[1]
    share = share.reshape(16, items // 16, width)

    below_n, above_f, near1, far1 = together(
        [
            (near, X_STEP[1]),
            (far, X_STEP[3]),
            (outer, NEAR),
            (inner, FAR),
        ]
    )
    below_f, above_n, two0, two1, right_c = together(
        [(far, X_STEP[1]), (near, X_STEP[3]), (far, NEAR), (near, FAR), (right, CORE)],
        (below_n, above_f),
    )
    rim = jnp.stack([near1, far1])
    rim_c, two0_c, two1_c = together(
        [(rim, CORE), (two0, CORE), (two1, CORE)], (below_f, above_n)
    )
    across = together([(below_n, X_STEP[1]), (above_f, X_STEP[3])], (below_f, above_n))
    side = (
        ((whole, "0"), two0),
        ((whole, "1"), two1),
        (near, far),
        (near1, far1),
    )
    side_c = (
        ((whole_c, "0"), two0_c),
        ((whole_c, "1"), two1_c),
        ((right_c, 0), (right_c, 1)),
        ((rim_c, 0), (rim_c, 1)),
    )
    early = {0: (near, far), 1: (above_n, above_f), 3: (below_n, below_f)}
    kept = block_product(place, {0: side}, early)
    kept = block_product(place, {1: side_c}, early, kept)
    across, kept = lax.optimization_barrier((across, kept))
    home, up, down, middle = block_product(
        place, {0: side, 1: side_c}, {2: tuple(across)}, kept
    )

    share, down, up = lax.optimization_barrier((share, down, up))
    shares = lax.all_to_all(share, "feat", 0, 0)
    down, up = together([(down, Z_STEP[3]), (up, Z_STEP[1])])
    first, second = together(
        [
            (narrow(wide(down[0]) + wide(middle[0])), Z_STEP[3]),
            (narrow(wide(up[1]) + wide(middle[1])), Z_STEP[1]),
        ]
    )
    total = [
        narrow(wide(home[0]) + wide(up[0]) + wide(first)).reshape(2, 2, half, half),
        narrow(wide(home[1]) + wide(down[1]) + wide(second)).reshape(2, 2, half, half),
    ]
    homeward = []
    for s in range(2):
        for t in range(2):
            chosen = pick(total[t], yl ^ yh ^ s)
            value = jnp.concatenate([pick(chosen, yh ^ i) for i in range(2)], 0)
            homeward.append(value)
    shares, homeward = lax.optimization_barrier((shares, homeward))
    projected = narrow(jnp.sum(wide(shares), 0))
    arrived = [send(v, HOME[s // 2, s % 2]) for s, v in enumerate(homeward)]
    *arrived, projected = lax.optimization_barrier((*arrived, projected))
    arrived = jnp.stack(arrived)
    gram = jnp.concatenate(
        [pick(arrived, (q % 2 ^ yl) * 2 + (q // 2 ^ c)) for q in range(4)], 1
    )
    covariance = 0.9 * cov_prior + wide(gram) / items_total
    return (covariance, projected)


def solution(mesh):
    placed = (P("batch", "feat"), P("feat", None), P("feat", "batch"))
    return jax.shard_map(
        on_device,
        mesh=mesh,
        in_specs=placed,
        out_specs=(P("feat", "batch"), P(("batch", "feat"), None)),
        check_vma=False,
    )
```

```python
import functools

import jax
import jax.numpy as jnp
from jax import lax
from jax.experimental import pallas as pl
from jax.experimental.pallas import tpu as pltpu
from jax.sharding import PartitionSpec as P

SIZES = (4, 2, 2, 4, 2)
AXES = ("feat", "batch")


def flat(place):
    index = 0
    for value, size in zip(place, SIZES):
        index = index * size + value % size
    return index


def table(move):
    pairs = []
    for x in range(4):
        for yl in range(2):
            for c in range(2):
                for z in range(4):
                    for yh in range(2):
                        pairs.append((flat((x, yl, c, z, yh)), flat(move(x, yl, c, z, yh))))
    return pairs


CORE = table(lambda x, yl, c, z, yh: (x, yl, 1 - c, z, yh))
NEAR = table(lambda x, yl, c, z, yh: (x, 1 - yl, c, z, yh))
FAR = table(lambda x, yl, c, z, yh: (x, 1 - yl, c, z, 1 - yh))
X_STEP = {d: table(lambda x, yl, c, z, yh, d=d: (x + d, yl, c, z, yh)) for d in (1, 2, 3)}
Z_STEP = {d: table(lambda x, yl, c, z, yh, d=d: (x, yl, c, z + d, yh)) for d in (1, 3)}
HOME = {
    (s, t): table(lambda x, yl, c, z, yh, s=s, t=t: (x, yh ^ s, c ^ t, z, 1 - yl))
    for s in range(2)
    for t in range(2)
}


def send(value, pairs):
    return lax.ppermute(value, AXES, pairs)


def pick(array, index):
    return lax.dynamic_index_in_dim(array, index, 0, keepdims=False)


def wide(value):
    return value.astype(jnp.float32)


def narrow(value):
    return value.astype(jnp.bfloat16)


def together(sends, after=()):
    values, _ = lax.optimization_barrier(([value for value, _ in sends], after))
    results = [send(value, pairs) for value, (_, pairs) in zip(values, sends)]
    return lax.optimization_barrier(results)


def block_kernel(plan, sides, *refs):
    place, refs = refs[0], refs[1:]
    n_in = plan["inputs"]
    inputs, refs = refs[:n_in], refs[n_in + plan["kept"] :]
    home, up, down, middle = refs[:4]
    targets, refs = ((home, up, down, middle), (home, middle, up, down)), refs[4:]
    left, columns_in, result, left_sem, column_sem, out_sem = refs
    shift, high = place[0], place[1]
    rows = columns_in.shape[2]

    def view(name):
        index, part = name
        if part is None:
            return inputs[index]
        return inputs[index].at[part if isinstance(part, int) else (high ^ int(part))]

    rights = [
        pltpu.make_async_copy(view(name), columns_in.at[n, i], column_sem.at[2 * n + i])
        for n, names in enumerate(plan["blocks"])
        for i, name in enumerate(names)
    ]
    lefts = [
        pltpu.make_async_copy(
            view(name),
            left.at[k // 4, i, pl.ds(k % 4 * rows, rows)],
            left_sem.at[2 * k + i],
        )
        for k, names in enumerate(sides)
        for i, name in enumerate(names)
    ]
    for copy in rights[:2] + lefts[:8] + rights[2:] + lefts[8:]:
        copy.start()
    outs = []
    arrived = set()
    for side, (cc, wanted) in enumerate(plan["sides"]):
        for copy in lefts[8 * side : 8 * side + 8]:
            copy.wait()
        for n, dx in wanted:
            if n not in arrived:
                arrived.add(n)
                for copy in rights[2 * n : 2 * n + 2]:
                    copy.wait()
            total = None
            for i in range(2):
                term = lax.dot_general(
                    left[side, i],
                    columns_in[n, i],
                    (((1,), (1,)), ((), ())),
                    preferred_element_type=jnp.float32,
                )
                total = term if total is None else total + term
            slot = len(outs) // 4
            result[slot] = total.astype(jnp.bfloat16)
            dz = (shift + dx) % 4
            for d in range(4):
                copy = pltpu.make_async_copy(
                    result.at[slot], targets[cc][d].at[cc], out_sem.at[slot]
                )
                outs.append((dz == d, copy))
                pl.when(dz == d)(copy.start)
    for here, copy in outs:
        pl.when(here)(copy.wait)


def block_product(place, sides, blocks, kept=()):
    inputs = []

    def enter(piece):
        array, part = piece if isinstance(piece, tuple) else (piece, None)
        for index, known in enumerate(inputs):
            if known is array:
                return index, part
        inputs.append(array)
        return len(inputs) - 1, part

    groups = [[enter(piece) for piece in pair] for side, _ in sides.values() for pair in side]
    names = [[enter(piece) for piece in pair] for pair in blocks.values()]
    half, items = inputs[0].shape[-2:]
    order = list(blocks)
    wanted = tuple((cc, tuple((order.index(dx), dx) for dx in dxs)) for cc, (_, dxs) in sides.items())
    n_results = sum(len(dxs) for _, dxs in wanted)
    plan = {"inputs": len(inputs), "kept": len(kept), "sides": wanted, "blocks": names}
    outside = pl.BlockSpec(memory_space=pltpu.HBM)
    n_blocks = len(blocks)
    return pl.pallas_call(
        functools.partial(block_kernel, plan, groups),
        out_shape=[jax.ShapeDtypeStruct((2, 4 * half, half), jnp.bfloat16)] * 4,
        in_specs=[pl.BlockSpec(memory_space=pltpu.SMEM)]
        + [outside] * (len(inputs) + len(kept)),
        out_specs=[outside] * 4,
        input_output_aliases={1 + len(inputs) + n: n for n in range(len(kept))},
        scratch_shapes=[
            pltpu.VMEM((len(sides), 2, 4 * half, items), jnp.bfloat16),
            pltpu.VMEM((n_blocks, 2, half, items), jnp.bfloat16),
            pltpu.VMEM((n_results, 4 * half, half), jnp.bfloat16),
            pltpu.SemaphoreType.DMA((2 * len(groups),)),
            pltpu.SemaphoreType.DMA((2 * n_blocks,)),
            pltpu.SemaphoreType.DMA((n_results,)),
        ],
        compiler_params=pltpu.CompilerParams(vmem_limit_bytes=60 * 1024 * 1024),
        cost_estimate=pl.CostEstimate(
            flops=half * half, bytes_accessed=half * items, transcendentals=0
        ),
    )(place, *inputs, *kept)


def on_device(embeddings, basis, cov_prior):
    feat, batch = lax.axis_index("feat"), lax.axis_index("batch")
    x, yl, c = feat // 4, feat // 2 % 2, feat % 2
    z, yh = batch // 2, batch % 2
    items, feats = embeddings.shape
    half = feats // 2
    items_total = items * lax.axis_size("batch")
    place = jnp.stack([(x - z) % 4, yh]).astype(jnp.int32)

    whole = embeddings.T.reshape(2, half, items)
    inner, outer = pick(whole, yh), pick(whole, 1 - yh)
    near, far, whole_c = together([(inner, NEAR), (outer, FAR), (whole, CORE)])
    right = jnp.stack([near, far])
    share = narrow(jnp.dot(embeddings, basis, preferred_element_type=jnp.float32))
    width = share.shape[1]
    share = share.reshape(16, items // 16, width)

    below_n, above_f, near1, far1 = together(
        [
            (near, X_STEP[1]),
            (far, X_STEP[3]),
            (outer, NEAR),
            (inner, FAR),
        ],
        (share,),
    )
    below_f, above_n, two0, two1, right_c = together(
        [(far, X_STEP[1]), (near, X_STEP[3]), (far, NEAR), (near, FAR), (right, CORE)],
        (below_n, above_f),
    )
    rim = jnp.stack([near1, far1])
    rim_c, two0_c, two1_c = together(
        [(rim, CORE), (two0, CORE), (two1, CORE)], (below_f, above_n)
    )
    across = together([(below_n, X_STEP[1]), (above_f, X_STEP[3])], (below_f, above_n))
    side = (
        ((whole, "0"), two0),
        ((whole, "1"), two1),
        (near, far),
        (near1, far1),
    )
    side_c = (
        ((whole_c, "0"), two0_c),
        ((whole_c, "1"), two1_c),
        ((right_c, 0), (right_c, 1)),
        ((rim_c, 0), (rim_c, 1)),
    )
    early = {0: (near, far), 1: (above_n, above_f), 3: (below_n, below_f)}
    kept = block_product(place, {0: (side, (0, 1, 3))}, early)
    home, up, down, middle = block_product(
        place, {1: (side_c, (0, 1, 3, 2)), 0: (side, (2,))}, {**early, 2: tuple(across)}, kept
    )

    share, down, up = lax.optimization_barrier((share, down, up))
    shares = lax.all_to_all(share, "feat", 0, 0)
    down, up = together([(down, Z_STEP[3]), (up, Z_STEP[1])])
    first, second = together(
        [
            (narrow(wide(down[0]) + wide(middle[0])), Z_STEP[3]),
            (narrow(wide(up[1]) + wide(middle[1])), Z_STEP[1]),
        ]
    )
    total = [
        narrow(wide(home[0]) + wide(up[0]) + wide(first)).reshape(2, 2, half, half),
        narrow(wide(home[1]) + wide(down[1]) + wide(second)).reshape(2, 2, half, half),
    ]
    homeward = []
    for s in range(2):
        for t in range(2):
            chosen = pick(total[t], yl ^ yh ^ s)
            value = jnp.concatenate([pick(chosen, yh ^ i) for i in range(2)], 0)
            homeward.append(value)
    shares, homeward = lax.optimization_barrier((shares, homeward))
    projected = narrow(jnp.sum(wide(shares), 0))
    arrived = [send(v, HOME[s // 2, s % 2]) for s, v in enumerate(homeward)]
    *arrived, projected = lax.optimization_barrier((*arrived, projected))
    arrived = jnp.stack(arrived)
    gram = jnp.concatenate(
        [pick(arrived, (q % 2 ^ yl) * 2 + (q // 2 ^ c)) for q in range(4)], 1
    )
    covariance = 0.9 * cov_prior + wide(gram) / items_total
    return (covariance, projected)


def solution(mesh):
    placed = (P("batch", "feat"), P("feat", None), P("feat", "batch"))
    return jax.shard_map(
        on_device,
        mesh=mesh,
        in_specs=placed,
        out_specs=(P("feat", "batch"), P(("batch", "feat"), None)),
        check_vma=False,
    )
```

```python
import functools

import jax
import jax.numpy as jnp
from jax import lax
from jax.experimental import pallas as pl
from jax.experimental.pallas import tpu as pltpu
from jax.sharding import PartitionSpec as P

SIZES = (4, 2, 2, 4, 2)
AXES = ("feat", "batch")
LATE = 60


def flat(place):
    index = 0
    for value, size in zip(place, SIZES):
        index = index * size + value % size
    return index


def table(move):
    pairs = []
    for x in range(4):
        for yl in range(2):
            for c in range(2):
                for z in range(4):
                    for yh in range(2):
                        pairs.append((flat((x, yl, c, z, yh)), flat(move(x, yl, c, z, yh))))
    return pairs


CORE = table(lambda x, yl, c, z, yh: (x, yl, 1 - c, z, yh))
NEAR = table(lambda x, yl, c, z, yh: (x, 1 - yl, c, z, yh))
FAR = table(lambda x, yl, c, z, yh: (x, 1 - yl, c, z, 1 - yh))
X_STEP = {d: table(lambda x, yl, c, z, yh, d=d: (x + d, yl, c, z, yh)) for d in (1, 2, 3)}
Z_STEP = {d: table(lambda x, yl, c, z, yh, d=d: (x, yl, c, z + d, yh)) for d in (1, 3)}
HOME = {
    (s, t): table(lambda x, yl, c, z, yh, s=s, t=t: (x, yh ^ s, c ^ t, z, 1 - yl))
    for s in range(2)
    for t in range(2)
}


def send(value, pairs):
    return lax.ppermute(value, AXES, pairs)


def pick(array, index):
    return lax.dynamic_index_in_dim(array, index, 0, keepdims=False)


def wide(value):
    return value.astype(jnp.float32)


def narrow(value):
    return value.astype(jnp.bfloat16)


def together(sends, after=()):
    values, _ = lax.optimization_barrier(([value for value, _ in sends], after))
    results = [send(value, pairs) for value, (_, pairs) in zip(values, sends)]
    return lax.optimization_barrier(results)


def block_kernel(plan, sides, *refs):
    place, refs = refs[0], refs[1:]
    n_in = plan["inputs"]
    inputs, refs = refs[:n_in], refs[n_in + plan["kept"] :]
    if plan["messages"] == 4:
        home, up, down, middle = refs[:4]
    else:
        (home, middle), up, down = refs[:2], None, None
    targets = ((home, up, down, middle), (home, middle, up, down))
    refs = refs[plan["messages"] :]
    left, columns_in, result, left_sem, column_sem, out_sem = refs
    shift, high = place[0], place[1]
    rows = columns_in.shape[2]

    def view(name):
        index, part = name
        if part is None:
            return inputs[index]
        return inputs[index].at[part if isinstance(part, int) else (high ^ int(part))]

    rights = [
        pltpu.make_async_copy(view(name), columns_in.at[n, i], column_sem.at[2 * n + i])
        for n, names in enumerate(plan["blocks"])
        for i, name in enumerate(names)
    ]
    lefts = [
        pltpu.make_async_copy(
            view(name),
            left.at[k // 4, i, pl.ds(k % 4 * rows, rows)],
            left_sem.at[2 * k + i],
        )
        for k, names in enumerate(sides)
        for i, name in enumerate(names)
    ]
    for copy in rights[:2] + lefts[:8] + rights[2:] + lefts[8:]:
        copy.start()
    outs = []
    arrived = set()
    slot = 0
    for side, (cc, wanted) in enumerate(plan["sides"]):
        for copy in lefts[8 * side : 8 * side + 8]:
            copy.wait()
        for kind, which in wanted:
            if kind == "dz":
                block = (which + 4 - shift) % 4
                needed = range(len(plan["blocks"]))
                options = [(None, which)]
            else:
                block = plan["order"].index(which)
                needed = (block,)
                dz = (shift + which) % 4
                options = [(dz == d, d) for d in range(4)]
            for n in needed:
                if n not in arrived:
                    arrived.add(n)
                    for copy in rights[2 * n : 2 * n + 2]:
                        copy.wait()
            total = None
            for i in range(2):
                term = lax.dot_general(
                    left[side, i],
                    columns_in[block, i],
                    (((1,), (1,)), ((), ())),
                    preferred_element_type=jnp.float32,
                )
                total = term if total is None else total + term
            result[slot] = total.astype(jnp.bfloat16)
            for here, d in options:
                copy = pltpu.make_async_copy(
                    result.at[slot], targets[cc][d].at[cc], out_sem.at[slot]
                )
                outs.append((here, copy))
                if here is None:
                    copy.start()
                else:
                    pl.when(here)(copy.start)
            slot += 1
    for here, copy in outs:
        if here is None:
            copy.wait()
        else:
            pl.when(here)(copy.wait)


def block_product(place, sides, blocks, kept=(), limit=60):
    inputs = []

    def enter(piece):
        array, part = piece if isinstance(piece, tuple) else (piece, None)
        for index, known in enumerate(inputs):
            if known is array:
                return index, part
        inputs.append(array)
        return len(inputs) - 1, part

    groups = [[enter(piece) for piece in pair] for side, _ in sides.values() for pair in side]
    names = [[enter(piece) for piece in pair] for pair in blocks.values()]
    half, items = inputs[0].shape[-2:]
    wanted = tuple((cc, jobs) for cc, (_, jobs) in sides.items())
    n_results = sum(len(jobs) for _, jobs in wanted)
    n_messages = len(kept) or 4
    plan = {
        "inputs": len(inputs),
        "kept": len(kept),
        "messages": n_messages,
        "sides": wanted,
        "blocks": names,
        "order": tuple(blocks),
    }
    outside = pl.BlockSpec(memory_space=pltpu.HBM)
    n_blocks = len(blocks)
    return pl.pallas_call(
        functools.partial(block_kernel, plan, groups),
        out_shape=[jax.ShapeDtypeStruct((2, 4 * half, half), jnp.bfloat16)] * n_messages,
        in_specs=[pl.BlockSpec(memory_space=pltpu.SMEM)]
        + [outside] * (len(inputs) + len(kept)),
        out_specs=[outside] * n_messages,
        input_output_aliases={1 + len(inputs) + n: n for n in range(len(kept))},
        scratch_shapes=[
            pltpu.VMEM((len(sides), 2, 4 * half, items), jnp.bfloat16),
            pltpu.VMEM((n_blocks, 2, half, items), jnp.bfloat16),
            pltpu.VMEM((n_results, 4 * half, half), jnp.bfloat16),
            pltpu.SemaphoreType.DMA((2 * len(groups),)),
            pltpu.SemaphoreType.DMA((2 * n_blocks,)),
            pltpu.SemaphoreType.DMA((n_results,)),
        ],
        compiler_params=pltpu.CompilerParams(vmem_limit_bytes=limit * 1024 * 1024),
        cost_estimate=pl.CostEstimate(
            flops=half * half, bytes_accessed=half * items, transcendentals=0
        ),
    )(place, *inputs, *kept)


def on_device(embeddings, basis, cov_prior):
    feat, batch = lax.axis_index("feat"), lax.axis_index("batch")
    x, yl, c = feat // 4, feat // 2 % 2, feat % 2
    z, yh = batch // 2, batch % 2
    items, feats = embeddings.shape
    half = feats // 2
    items_total = items * lax.axis_size("batch")
    place = jnp.stack([(x - z) % 4, yh]).astype(jnp.int32)

    whole = embeddings.T.reshape(2, half, items)
    inner, outer = pick(whole, yh), pick(whole, 1 - yh)
    near, far, whole_c = together([(inner, NEAR), (outer, FAR), (whole, CORE)])
    right = jnp.stack([near, far])
    share = narrow(jnp.dot(embeddings, basis, preferred_element_type=jnp.float32))
    width = share.shape[1]
    share = share.reshape(16, items // 16, width)

    below_n, above_f, near1, far1 = together(
        [
            (near, X_STEP[1]),
            (far, X_STEP[3]),
            (outer, NEAR),
            (inner, FAR),
        ],
        (share,),
    )
    below_f, above_n, two0, two1, right_c = together(
        [(far, X_STEP[1]), (near, X_STEP[3]), (far, NEAR), (near, FAR), (right, CORE)],
        (below_n, above_f),
    )
    rim = jnp.stack([near1, far1])
    rim_c, two0_c, two1_c = together(
        [(rim, CORE), (two0, CORE), (two1, CORE)], (below_f, above_n)
    )
    across = together([(below_n, X_STEP[1]), (above_f, X_STEP[3])], (below_f, above_n))
    side = (
        ((whole, "0"), two0),
        ((whole, "1"), two1),
        (near, far),
        (near1, far1),
    )
    side_c = (
        ((whole_c, "0"), two0_c),
        ((whole_c, "1"), two1_c),
        ((right_c, 0), (right_c, 1)),
        ((rim_c, 0), (rim_c, 1)),
    )
    early = {0: (near, far), 1: (above_n, above_f), 3: (below_n, below_f)}
    every = {0: (near, far), 1: (above_n, above_f), 2: tuple(across), 3: (below_n, below_f)}
    kept = block_product(place, {0: (side, (("dx", 0), ("dx", 1), ("dx", 3)))}, early)
    home, up, down, middle = block_product(
        place, {1: (side_c, (("dz", 2), ("dz", 3))), 0: (side, (("dx", 2),))}, every, kept
    )
    home, middle = block_product(
        place, {1: (side_c, (("dz", 1), ("dz", 0)))}, every, (home, middle), LATE
    )

    share, down, up = lax.optimization_barrier((share, down, up))
    shares = lax.all_to_all(share, "feat", 0, 0)
    down, up = together([(down, Z_STEP[3]), (up, Z_STEP[1])])
    first, second = together(
        [
            (narrow(wide(down[0]) + wide(middle[0])), Z_STEP[3]),
            (narrow(wide(up[1]) + wide(middle[1])), Z_STEP[1]),
        ]
    )
    total = [
        narrow(wide(home[0]) + wide(up[0]) + wide(first)).reshape(2, 2 * half, half),
        narrow(wide(home[1]) + wide(down[1]) + wide(second)).reshape(2, 2 * half, half),
    ]
    homeward = [pick(total[t], yl ^ yh ^ s) for s in range(2) for t in range(2)]
    shares, homeward = lax.optimization_barrier((shares, homeward))
    projected = narrow(jnp.sum(wide(shares), 0))
    arrived = [send(v, HOME[s // 2, s % 2]) for s, v in enumerate(homeward)]
    *arrived, projected = lax.optimization_barrier((*arrived, projected))

    def quarter(q):
        t, s = q // 2, q % 2
        value = jnp.where(
            c == 0,
            jnp.where(yl == 0, arrived[2 * s + t], arrived[2 - 2 * s + t]),
            jnp.where(yl == 0, arrived[2 * s + 1 - t], arrived[3 - 2 * s - t]),
        )
        return jnp.concatenate([value[half:], value[:half]], 0) if s else value

    gram = jnp.concatenate([quarter(q) for q in range(4)], 1)
    covariance = 0.9 * cov_prior + wide(gram) / items_total
    return (covariance, projected)


def solution(mesh):
    placed = (P("batch", "feat"), P("feat", None), P("feat", "batch"))
    return jax.shard_map(
        on_device,
        mesh=mesh,
        in_specs=placed,
        out_specs=(P("feat", "batch"), P(("batch", "feat"), None)),
        check_vma=False,
    )
```

```python
import functools

import jax
import jax.numpy as jnp
from jax import lax
from jax.experimental import pallas as pl
from jax.experimental.pallas import tpu as pltpu
from jax.sharding import PartitionSpec as P

SIZES = (4, 2, 2, 4, 2)
AXES = ("feat", "batch")
LATE = 60


def flat(place):
    index = 0
    for value, size in zip(place, SIZES):
        index = index * size + value % size
    return index


def table(move):
    pairs = []
    for x in range(4):
        for yl in range(2):
            for c in range(2):
                for z in range(4):
                    for yh in range(2):
                        pairs.append((flat((x, yl, c, z, yh)), flat(move(x, yl, c, z, yh))))
    return pairs


CORE = table(lambda x, yl, c, z, yh: (x, yl, 1 - c, z, yh))
NEAR = table(lambda x, yl, c, z, yh: (x, 1 - yl, c, z, yh))
FAR = table(lambda x, yl, c, z, yh: (x, 1 - yl, c, z, 1 - yh))
X_STEP = {d: table(lambda x, yl, c, z, yh, d=d: (x + d, yl, c, z, yh)) for d in (1, 2, 3)}
Z_STEP = {d: table(lambda x, yl, c, z, yh, d=d: (x, yl, c, z + d, yh)) for d in (1, 3)}
HOME = {
    (s, t): table(lambda x, yl, c, z, yh, s=s, t=t: (x, yh ^ s, c ^ t, z, 1 - yl))
    for s in range(2)
    for t in range(2)
}


def send(value, pairs):
    return lax.ppermute(value, AXES, pairs)


def pick(array, index):
    return lax.dynamic_index_in_dim(array, index, 0, keepdims=False)


def wide(value):
    return value.astype(jnp.float32)


def narrow(value):
    return value.astype(jnp.bfloat16)


def together(sends, after=()):
    values, _ = lax.optimization_barrier(([value for value, _ in sends], after))
    results = [send(value, pairs) for value, (_, pairs) in zip(values, sends)]
    return lax.optimization_barrier(results)


def block_kernel(plan, sides, *refs):
    place, refs = refs[0], refs[1:]
    n_in = plan["inputs"]
    inputs, refs = refs[:n_in], refs[n_in + plan["kept"] :]
    if plan["messages"] == 4:
        home, up, down, middle = refs[:4]
    else:
        (home, middle), up, down = refs[:2], None, None
    targets = ((home, up, down, middle), (home, middle, up, down))
    refs = refs[plan["messages"] :]
    left, columns_in, result, left_sem, column_sem, out_sem = refs
    shift, high = place[0], place[1]
    rows = columns_in.shape[2]

    def view(name):
        index, part = name
        if part is None:
            return inputs[index]
        return inputs[index].at[part if isinstance(part, int) else (high ^ int(part))]

    jobs = [
        (side, cc, kind, which)
        for side, (cc, wanted) in enumerate(plan["sides"])
        for kind, which in wanted
    ]
    rights = []
    for slot, (_, _, kind, which) in enumerate(jobs):
        if kind == "dx":
            options = [(None, which)]
        else:
            dx = (which + 4 - shift) % 4
            options = [(dx == k, k) for k in plan["order"]]
        rights.append(
            [
                (
                    here,
                    pltpu.make_async_copy(
                        view(plan["blocks"][plan["order"].index(k)][i]),
                        columns_in.at[slot, i],
                        column_sem.at[2 * slot + i],
                    ),
                )
                for here, k in options
                for i in range(2)
            ]
        )
    lefts = [
        pltpu.make_async_copy(
            view(name),
            left.at[k // 4, i, pl.ds(k % 4 * rows, rows)],
            left_sem.at[2 * k + i],
        )
        for k, names in enumerate(sides)
        for i, name in enumerate(names)
    ]

    def each(copies, act):
        for here, copy in copies:
            if here is None:
                getattr(copy, act)()
            else:
                pl.when(here)(getattr(copy, act))

    for slot, (side, *_) in enumerate(jobs):
        each(rights[slot], "start")
        if slot == 0 or jobs[slot - 1][0] != side:
            each([(None, copy) for copy in lefts[8 * side : 8 * side + 8]], "start")
    outs = []
    for slot, (side, cc, kind, which) in enumerate(jobs):
        if slot == 0 or jobs[slot - 1][0] != side:
            each([(None, copy) for copy in lefts[8 * side : 8 * side + 8]], "wait")
        each(rights[slot], "wait")
        total = None
        for i in range(2):
            term = lax.dot_general(
                left[side, i],
                columns_in[slot, i],
                (((1,), (1,)), ((), ())),
                preferred_element_type=jnp.float32,
            )
            total = term if total is None else total + term
        result[slot] = total.astype(jnp.bfloat16)
        dz = (shift + which) % 4
        options = [(dz == d, d) for d in range(4)] if kind == "dx" else [(None, which)]
        copies = [
            (
                here,
                pltpu.make_async_copy(
                    result.at[slot], targets[cc][d].at[cc], out_sem.at[slot]
                ),
            )
            for here, d in options
        ]
        each(copies, "start")
        outs += copies
    each(outs, "wait")


def block_product(place, sides, blocks, kept=(), limit=60):
    inputs = []

    def enter(piece):
        array, part = piece if isinstance(piece, tuple) else (piece, None)
        for index, known in enumerate(inputs):
            if known is array:
                return index, part
        inputs.append(array)
        return len(inputs) - 1, part

    groups = [[enter(piece) for piece in pair] for side, _ in sides.values() for pair in side]
    names = [[enter(piece) for piece in pair] for pair in blocks.values()]
    half, items = inputs[0].shape[-2:]
    wanted = tuple((cc, jobs) for cc, (_, jobs) in sides.items())
    n_results = sum(len(jobs) for _, jobs in wanted)
    n_messages = len(kept) or 4
    plan = {
        "inputs": len(inputs),
        "kept": len(kept),
        "messages": n_messages,
        "sides": wanted,
        "blocks": names,
        "order": tuple(blocks),
    }
    outside = pl.BlockSpec(memory_space=pltpu.HBM)
    n_blocks = len(blocks)
    return pl.pallas_call(
        functools.partial(block_kernel, plan, groups),
        out_shape=[jax.ShapeDtypeStruct((2, 4 * half, half), jnp.bfloat16)] * n_messages,
        in_specs=[pl.BlockSpec(memory_space=pltpu.SMEM)]
        + [outside] * (len(inputs) + len(kept)),
        out_specs=[outside] * n_messages,
        input_output_aliases={1 + len(inputs) + n: n for n in range(len(kept))},
        scratch_shapes=[
            pltpu.VMEM((len(sides), 2, 4 * half, items), jnp.bfloat16),
            pltpu.VMEM((n_results, 2, half, items), jnp.bfloat16),
            pltpu.VMEM((n_results, 4 * half, half), jnp.bfloat16),
            pltpu.SemaphoreType.DMA((2 * len(groups),)),
            pltpu.SemaphoreType.DMA((2 * n_results,)),
            pltpu.SemaphoreType.DMA((n_results,)),
        ],
        compiler_params=pltpu.CompilerParams(vmem_limit_bytes=limit * 1024 * 1024),
        cost_estimate=pl.CostEstimate(
            flops=half * half, bytes_accessed=half * items, transcendentals=0
        ),
    )(place, *inputs, *kept)


def on_device(embeddings, basis, cov_prior):
    feat, batch = lax.axis_index("feat"), lax.axis_index("batch")
    x, yl, c = feat // 4, feat // 2 % 2, feat % 2
    z, yh = batch // 2, batch % 2
    items, feats = embeddings.shape
    half = feats // 2
    items_total = items * lax.axis_size("batch")
    place = jnp.stack([(x - z) % 4, yh]).astype(jnp.int32)

    whole = embeddings.T.reshape(2, half, items)
    inner, outer = pick(whole, yh), pick(whole, 1 - yh)
    near, far, whole_c = together([(inner, NEAR), (outer, FAR), (whole, CORE)])
    right = jnp.stack([near, far])
    share = narrow(jnp.dot(embeddings, basis, preferred_element_type=jnp.float32))
    width = share.shape[1]
    share = share.reshape(16, items // 16, width)

    below_n, above_f = together([(near, X_STEP[1]), (far, X_STEP[3])], (share,))
    near1, far1 = together([(outer, NEAR), (inner, FAR)], (near, far, share))
    below_f, above_n = together([(far, X_STEP[1]), (near, X_STEP[3])], (below_n, above_f))
    two0, two1, right_c = together(
        [(far, NEAR), (near, FAR), (right, CORE)], (near1, far1)
    )
    rim = jnp.stack([near1, far1])
    across = together([(below_n, X_STEP[1]), (above_f, X_STEP[3])], (below_f, above_n))
    (rim_c,) = together([(rim, CORE)])
    two0_c, two1_c = together([(two0, CORE), (two1, CORE)])
    side = (
        ((whole, "0"), two0),
        ((whole, "1"), two1),
        (near, far),
        (near1, far1),
    )
    side_c = (
        ((whole_c, "0"), two0_c),
        ((whole_c, "1"), two1_c),
        ((right_c, 0), (right_c, 1)),
        ((rim_c, 0), (rim_c, 1)),
    )
    early = {0: (near, far), 1: (above_n, above_f), 3: (below_n, below_f)}
    every = {0: (near, far), 1: (above_n, above_f), 2: tuple(across), 3: (below_n, below_f)}
    kept = block_product(place, {0: (side, (("dx", 0), ("dx", 1), ("dx", 3)))}, early)
    home, up, down, middle = block_product(
        place, {1: (side_c, (("dz", 2), ("dz", 3))), 0: (side, (("dx", 2),))}, every, kept
    )
    home, middle = block_product(
        place, {1: (side_c, (("dz", 1), ("dz", 0)))}, every, (home, middle), LATE
    )

    share, down, up = lax.optimization_barrier((share, down, up))
    shares = lax.all_to_all(share, "feat", 0, 0)
    down, up = together([(down, Z_STEP[3]), (up, Z_STEP[1])])
    first, second = together(
        [
            (narrow(wide(down[0]) + wide(middle[0])), Z_STEP[3]),
            (narrow(wide(up[1]) + wide(middle[1])), Z_STEP[1]),
        ]
    )
    total = [
        narrow(wide(home[0]) + wide(up[0]) + wide(first)).reshape(2, 2 * half, half),
        narrow(wide(home[1]) + wide(down[1]) + wide(second)).reshape(2, 2 * half, half),
    ]
    homeward = [pick(total[t], yl ^ yh ^ s) for s in range(2) for t in range(2)]
    shares, homeward = lax.optimization_barrier((shares, homeward))
    projected = narrow(jnp.sum(wide(shares), 0))
    arrived = [send(v, HOME[s // 2, s % 2]) for s, v in enumerate(homeward)]
    *arrived, projected = lax.optimization_barrier((*arrived, projected))

    def quarter(q):
        t, s = q // 2, q % 2
        value = jnp.where(
            c == 0,
            jnp.where(yl == 0, arrived[2 * s + t], arrived[2 - 2 * s + t]),
            jnp.where(yl == 0, arrived[2 * s + 1 - t], arrived[3 - 2 * s - t]),
        )
        return jnp.concatenate([value[half:], value[:half]], 0) if s else value

    gram = jnp.concatenate([quarter(q) for q in range(4)], 1)
    covariance = 0.9 * cov_prior + wide(gram) / items_total
    return (covariance, projected)


def solution(mesh):
    placed = (P("batch", "feat"), P("feat", None), P("feat", "batch"))
    return jax.shard_map(
        on_device,
        mesh=mesh,
        in_specs=placed,
        out_specs=(P("feat", "batch"), P(("batch", "feat"), None)),
        check_vma=False,
    )
```

```python
import functools

import jax
import jax.numpy as jnp
from jax import lax
from jax.experimental import pallas as pl
from jax.experimental.pallas import tpu as pltpu
from jax.sharding import PartitionSpec as P

SIZES = (4, 2, 2, 4, 2)
AXES = ("feat", "batch")
LATE = 60


def flat(place):
    index = 0
    for value, size in zip(place, SIZES):
        index = index * size + value % size
    return index


def table(move):
    pairs = []
    for x in range(4):
        for yl in range(2):
            for c in range(2):
                for z in range(4):
                    for yh in range(2):
                        pairs.append((flat((x, yl, c, z, yh)), flat(move(x, yl, c, z, yh))))
    return pairs


CORE = table(lambda x, yl, c, z, yh: (x, yl, 1 - c, z, yh))
NEAR = table(lambda x, yl, c, z, yh: (x, 1 - yl, c, z, yh))
FAR = table(lambda x, yl, c, z, yh: (x, 1 - yl, c, z, 1 - yh))
X_STEP = {d: table(lambda x, yl, c, z, yh, d=d: (x + d, yl, c, z, yh)) for d in (1, 2, 3)}
Z_STEP = {d: table(lambda x, yl, c, z, yh, d=d: (x, yl, c, z + d, yh)) for d in (1, 3)}
HOME = {
    (s, t): table(lambda x, yl, c, z, yh, s=s, t=t: (x, yh ^ s, c ^ t, z, 1 - yl))
    for s in range(2)
    for t in range(2)
}


def send(value, pairs):
    return lax.ppermute(value, AXES, pairs)


def pick(array, index):
    return lax.dynamic_index_in_dim(array, index, 0, keepdims=False)


def wide(value):
    return value.astype(jnp.float32)


def narrow(value):
    return value.astype(jnp.bfloat16)


def together(sends, after=()):
    values, _ = lax.optimization_barrier(([value for value, _ in sends], after))
    results = [send(value, pairs) for value, (_, pairs) in zip(values, sends)]
    return lax.optimization_barrier(results)


def block_kernel(plan, sides, *refs):
    place, refs = refs[0], refs[1:]
    n_in = plan["inputs"]
    inputs, refs = refs[:n_in], refs[n_in + plan["kept"] :]
    if plan["messages"] == 4:
        home, up, down, middle = refs[:4]
    else:
        (home, middle), up, down = refs[:2], None, None
    targets = ((home, up, down, middle), (home, middle, up, down))
    refs = refs[plan["messages"] :]
    left, columns_in, result, left_sem, column_sem, out_sem = refs
    shift, high = place[0], place[1]
    rows = columns_in.shape[2]

    def view(name):
        index, part = name
        if part is None:
            return inputs[index]
        return inputs[index].at[part if isinstance(part, int) else (high ^ int(part))]

    jobs = [
        (side, cc, kind, which)
        for side, (cc, wanted) in enumerate(plan["sides"])
        for kind, which in wanted
    ]
    rights = []
    for slot, (_, _, kind, which) in enumerate(jobs):
        if kind == "dx":
            options = [(None, which)]
        else:
            dx = (which + 4 - shift) % 4
            options = [(dx == k, k) for k in plan["order"]]
        rights.append(
            [
                (
                    here,
                    pltpu.make_async_copy(
                        view(plan["blocks"][plan["order"].index(k)][i]),
                        columns_in.at[slot, i],
                        column_sem.at[2 * slot + i],
                    ),
                )
                for here, k in options
                for i in range(2)
            ]
        )
    lefts = [
        pltpu.make_async_copy(
            view(name),
            left.at[k // 4, i, pl.ds(k % 4 * rows, rows)],
            left_sem.at[2 * k + i],
        )
        for k, names in enumerate(sides)
        for i, name in enumerate(names)
    ]

    def each(copies, act):
        for here, copy in copies:
            if here is None:
                getattr(copy, act)()
            else:
                pl.when(here)(getattr(copy, act))

    for slot, (side, *_) in enumerate(jobs):
        each(rights[slot], "start")
        if slot == 0 or jobs[slot - 1][0] != side:
            each([(None, copy) for copy in lefts[8 * side : 8 * side + 8]], "start")
    outs = []
    for side, (cc, wanted) in enumerate(plan["sides"]):
        slots = [slot for slot, job in enumerate(jobs) if job[0] == side]
        each([(None, copy) for copy in lefts[8 * side : 8 * side + 8]], "wait")
        for slot in slots:
            each(rights[slot], "wait")

        def multiply(slot, carry):
            for group in range(4):
                here = slice(group * rows, (group + 1) * rows)
                total = None
                for i in range(2):
                    term = lax.dot_general(
                        left[side, i, here],
                        columns_in[slot, i],
                        (((1,), (1,)), ((), ())),
                        preferred_element_type=jnp.float32,
                    )
                    total = term if total is None else total + term
                result[slot, here] = total.astype(jnp.bfloat16)
            return carry

        lax.fori_loop(slots[0], slots[-1] + 1, multiply, 0)
        for slot, (kind, which) in zip(slots, wanted):
            dz = (shift + which) % 4
            options = [(dz == d, d) for d in range(4)] if kind == "dx" else [(None, which)]
            copies = [
                (
                    here,
                    pltpu.make_async_copy(
                        result.at[slot], targets[cc][d].at[cc], out_sem.at[slot]
                    ),
                )
                for here, d in options
            ]
            each(copies, "start")
            outs += copies
    each(outs, "wait")


def block_product(place, sides, blocks, kept=(), limit=60):
    inputs = []

    def enter(piece):
        array, part = piece if isinstance(piece, tuple) else (piece, None)
        for index, known in enumerate(inputs):
            if known is array:
                return index, part
        inputs.append(array)
        return len(inputs) - 1, part

    groups = [[enter(piece) for piece in pair] for side, _ in sides.values() for pair in side]
    names = [[enter(piece) for piece in pair] for pair in blocks.values()]
    half, items = inputs[0].shape[-2:]
    wanted = tuple((cc, jobs) for cc, (_, jobs) in sides.items())
    n_results = sum(len(jobs) for _, jobs in wanted)
    n_messages = len(kept) or 4
    plan = {
        "inputs": len(inputs),
        "kept": len(kept),
        "messages": n_messages,
        "sides": wanted,
        "blocks": names,
        "order": tuple(blocks),
    }
    outside = pl.BlockSpec(memory_space=pltpu.HBM)
    n_blocks = len(blocks)
    return pl.pallas_call(
        functools.partial(block_kernel, plan, groups),
        out_shape=[jax.ShapeDtypeStruct((2, 4 * half, half), jnp.bfloat16)] * n_messages,
        in_specs=[pl.BlockSpec(memory_space=pltpu.SMEM)]
        + [outside] * (len(inputs) + len(kept)),
        out_specs=[outside] * n_messages,
        input_output_aliases={1 + len(inputs) + n: n for n in range(len(kept))},
        scratch_shapes=[
            pltpu.VMEM((len(sides), 2, 4 * half, items), jnp.bfloat16),
            pltpu.VMEM((n_results, 2, half, items), jnp.bfloat16),
            pltpu.VMEM((n_results, 4 * half, half), jnp.bfloat16),
            pltpu.SemaphoreType.DMA((2 * len(groups),)),
            pltpu.SemaphoreType.DMA((2 * n_results,)),
            pltpu.SemaphoreType.DMA((n_results,)),
        ],
        compiler_params=pltpu.CompilerParams(vmem_limit_bytes=limit * 1024 * 1024),
        cost_estimate=pl.CostEstimate(
            flops=half * half, bytes_accessed=half * items, transcendentals=0
        ),
    )(place, *inputs, *kept)


def on_device(embeddings, basis, cov_prior):
    feat, batch = lax.axis_index("feat"), lax.axis_index("batch")
    x, yl, c = feat // 4, feat // 2 % 2, feat % 2
    z, yh = batch // 2, batch % 2
    items, feats = embeddings.shape
    half = feats // 2
    items_total = items * lax.axis_size("batch")
    place = jnp.stack([(x - z) % 4, yh]).astype(jnp.int32)

    whole = embeddings.T.reshape(2, half, items)
    inner, outer = pick(whole, yh), pick(whole, 1 - yh)
    near, far, whole_c = together([(inner, NEAR), (outer, FAR), (whole, CORE)])
    right = jnp.stack([near, far])
    share = narrow(jnp.dot(embeddings, basis, preferred_element_type=jnp.float32))
    width = share.shape[1]
    share = share.reshape(16, items // 16, width)

    below_n, above_f = together([(near, X_STEP[1]), (far, X_STEP[3])], (share,))
    near1, far1 = together([(outer, NEAR), (inner, FAR)], (near, far, share))
    below_f, above_n = together([(far, X_STEP[1]), (near, X_STEP[3])], (below_n, above_f))
    two0, two1, right_c = together(
        [(far, NEAR), (near, FAR), (right, CORE)], (near1, far1)
    )
    rim = jnp.stack([near1, far1])
    across = together([(below_n, X_STEP[1]), (above_f, X_STEP[3])], (below_f, above_n))
    (rim_c,) = together([(rim, CORE)])
    two0_c, two1_c = together([(two0, CORE), (two1, CORE)])
    side = (
        ((whole, "0"), two0),
        ((whole, "1"), two1),
        (near, far),
        (near1, far1),
    )
    side_c = (
        ((whole_c, "0"), two0_c),
        ((whole_c, "1"), two1_c),
        ((right_c, 0), (right_c, 1)),
        ((rim_c, 0), (rim_c, 1)),
    )
    early = {0: (near, far), 1: (above_n, above_f), 3: (below_n, below_f)}
    every = {0: (near, far), 1: (above_n, above_f), 2: tuple(across), 3: (below_n, below_f)}
    kept = block_product(place, {0: (side, (("dx", 0), ("dx", 1), ("dx", 3)))}, early)
    home, up, down, middle = block_product(
        place, {1: (side_c, (("dz", 2), ("dz", 3))), 0: (side, (("dx", 2),))}, every, kept
    )
    home, middle = block_product(
        place, {1: (side_c, (("dz", 1), ("dz", 0)))}, every, (home, middle), LATE
    )

    share, down, up = lax.optimization_barrier((share, down, up))
    shares = lax.all_to_all(share, "feat", 0, 0)
    down, up = together([(down, Z_STEP[3]), (up, Z_STEP[1])])
    first, second = together(
        [
            (narrow(wide(down[0]) + wide(middle[0])), Z_STEP[3]),
            (narrow(wide(up[1]) + wide(middle[1])), Z_STEP[1]),
        ]
    )
    total = [
        narrow(wide(home[0]) + wide(up[0]) + wide(first)).reshape(2, 2 * half, half),
        narrow(wide(home[1]) + wide(down[1]) + wide(second)).reshape(2, 2 * half, half),
    ]
    homeward = [pick(total[t], yl ^ yh ^ s) for s in range(2) for t in range(2)]
    shares, homeward = lax.optimization_barrier((shares, homeward))
    projected = narrow(jnp.sum(wide(shares), 0))
    arrived = [send(v, HOME[s // 2, s % 2]) for s, v in enumerate(homeward)]
    *arrived, projected = lax.optimization_barrier((*arrived, projected))

    def quarter(q):
        t, s = q // 2, q % 2
        value = jnp.where(
            c == 0,
            jnp.where(yl == 0, arrived[2 * s + t], arrived[2 - 2 * s + t]),
            jnp.where(yl == 0, arrived[2 * s + 1 - t], arrived[3 - 2 * s - t]),
        )
        return jnp.concatenate([value[half:], value[:half]], 0) if s else value

    gram = jnp.concatenate([quarter(q) for q in range(4)], 1)
    covariance = 0.9 * cov_prior + wide(gram) / items_total
    return (covariance, projected)


def solution(mesh):
    placed = (P("batch", "feat"), P("feat", None), P("feat", "batch"))
    return jax.shard_map(
        on_device,
        mesh=mesh,
        in_specs=placed,
        out_specs=(P("feat", "batch"), P(("batch", "feat"), None)),
        check_vma=False,
    )
```

```python
import functools

import jax
import jax.numpy as jnp
from jax import lax
from jax.experimental import pallas as pl
from jax.experimental.pallas import tpu as pltpu
from jax.sharding import PartitionSpec as P

SIZES = (4, 2, 2, 4, 2)
AXES = ("feat", "batch")
LATE = 60


def flat(place):
    index = 0
    for value, size in zip(place, SIZES):
        index = index * size + value % size
    return index


def table(move):
    pairs = []
    for x in range(4):
        for yl in range(2):
            for c in range(2):
                for z in range(4):
                    for yh in range(2):
                        pairs.append((flat((x, yl, c, z, yh)), flat(move(x, yl, c, z, yh))))
    return pairs


CORE = table(lambda x, yl, c, z, yh: (x, yl, 1 - c, z, yh))
NEAR = table(lambda x, yl, c, z, yh: (x, 1 - yl, c, z, yh))
FAR = table(lambda x, yl, c, z, yh: (x, 1 - yl, c, z, 1 - yh))
X_STEP = {d: table(lambda x, yl, c, z, yh, d=d: (x + d, yl, c, z, yh)) for d in (1, 2, 3)}
Z_STEP = {d: table(lambda x, yl, c, z, yh, d=d: (x, yl, c, z + d, yh)) for d in (1, 3)}
Z_CROSS = {d: table(lambda x, yl, c, z, yh, d=d: (x, yl, 1 - c, z + d, yh)) for d in (1, 3)}
HOME = [table(lambda x, yl, c, z, yh, s=s: (x, yh ^ s, c, z, 1 - yl)) for s in range(2)]


def send(value, pairs):
    return lax.ppermute(value, AXES, pairs)


def pick(array, index):
    return lax.dynamic_index_in_dim(array, index, 0, keepdims=False)


def wide(value):
    return value.astype(jnp.float32)


def narrow(value):
    return value.astype(jnp.bfloat16)


def together(sends, after=()):
    values, _ = lax.optimization_barrier(([value for value, _ in sends], after))
    results = [send(value, pairs) for value, (_, pairs) in zip(values, sends)]
    return lax.optimization_barrier(results)


def block_kernel(plan, sides, *refs):
    place, refs = refs[0], refs[1:]
    n_in = plan["inputs"]
    inputs, refs = refs[:n_in], refs[n_in + plan["kept"] :]
    if plan["messages"] == 6:
        home_a, home_b, up, down_a, down_b, middle = refs[:6]
        targets = (
            (home_a, up.at[0], down_a, middle.at[0]),
            (home_b, middle.at[1], up.at[1], down_b),
        )
    else:
        home_b, middle = refs[:2]
        targets = ((), (home_b, middle.at[1]))
    refs = refs[plan["messages"] :]
    left, columns_in, result, left_sem, column_sem, out_sem = refs
    shift, high = place[0], place[1]
    rows = columns_in.shape[2]

    def view(name):
        index, part = name
        if part is None:
            return inputs[index]
        return inputs[index].at[part if isinstance(part, int) else (high ^ int(part))]

    jobs = [
        (side, cc, kind, which)
        for side, (cc, wanted) in enumerate(plan["sides"])
        for kind, which in wanted
    ]
    rights = []
    for slot, (_, _, kind, which) in enumerate(jobs):
        if kind == "dx":
            options = [(None, which)]
        else:
            dx = (which + 4 - shift) % 4
            options = [(dx == k, k) for k in plan["order"]]
        rights.append(
            [
                (
                    here,
                    pltpu.make_async_copy(
                        view(plan["blocks"][plan["order"].index(k)][i]),
                        columns_in.at[slot, i],
                        column_sem.at[2 * slot + i],
                    ),
                )
                for here, k in options
                for i in range(2)
            ]
        )
    lefts = [
        pltpu.make_async_copy(
            view(name),
            left.at[k // 4, i, pl.ds(k % 4 * rows, rows)],
            left_sem.at[2 * k + i],
        )
        for k, names in enumerate(sides)
        for i, name in enumerate(names)
    ]

    def each(copies, act):
        for here, copy in copies:
            if here is None:
                getattr(copy, act)()
            else:
                pl.when(here)(getattr(copy, act))

    for slot, (side, *_) in enumerate(jobs):
        each(rights[slot], "start")
        if slot == 0 or jobs[slot - 1][0] != side:
            each([(None, copy) for copy in lefts[8 * side : 8 * side + 8]], "start")
    outs = []
    for side, (cc, wanted) in enumerate(plan["sides"]):
        slots = [slot for slot, job in enumerate(jobs) if job[0] == side]
        each([(None, copy) for copy in lefts[8 * side : 8 * side + 8]], "wait")
        for slot in slots:
            each(rights[slot], "wait")

        def multiply(slot, carry):
            for group in range(4):
                here = slice(group * rows, (group + 1) * rows)
                total = None
                for i in range(2):
                    term = lax.dot_general(
                        left[side, i, here],
                        columns_in[slot, i],
                        (((1,), (1,)), ((), ())),
                        preferred_element_type=jnp.float32,
                    )
                    total = term if total is None else total + term
                result[slot, here] = total.astype(jnp.bfloat16)
            return carry

        lax.fori_loop(slots[0], slots[-1] + 1, multiply, 0)
        for slot, (kind, which) in zip(slots, wanted):
            dz = (shift + which) % 4
            options = [(dz == d, d) for d in range(4)] if kind == "dx" else [(None, which)]
            copies = [
                (
                    here,
                    pltpu.make_async_copy(
                        result.at[slot], targets[cc][d], out_sem.at[slot]
                    ),
                )
                for here, d in options
            ]
            each(copies, "start")
            outs += copies
    each(outs, "wait")


def block_product(place, sides, blocks, kept=(), limit=60):
    inputs = []

    def enter(piece):
        array, part = piece if isinstance(piece, tuple) else (piece, None)
        for index, known in enumerate(inputs):
            if known is array:
                return index, part
        inputs.append(array)
        return len(inputs) - 1, part

    groups = [[enter(piece) for piece in pair] for side, _ in sides.values() for pair in side]
    names = [[enter(piece) for piece in pair] for pair in blocks.values()]
    half, items = inputs[0].shape[-2:]
    wanted = tuple((cc, jobs) for cc, (_, jobs) in sides.items())
    n_results = sum(len(jobs) for _, jobs in wanted)
    single = jax.ShapeDtypeStruct((4 * half, half), jnp.bfloat16)
    double = jax.ShapeDtypeStruct((2, 4 * half, half), jnp.bfloat16)
    messages = [single, single, double, single, single, double]
    if len(kept) == 2:
        messages = [single, double]
    n_messages = len(messages)
    plan = {
        "inputs": len(inputs),
        "kept": len(kept),
        "messages": n_messages,
        "sides": wanted,
        "blocks": names,
        "order": tuple(blocks),
    }
    outside = pl.BlockSpec(memory_space=pltpu.HBM)
    n_blocks = len(blocks)
    return pl.pallas_call(
        functools.partial(block_kernel, plan, groups),
        out_shape=messages,
        in_specs=[pl.BlockSpec(memory_space=pltpu.SMEM)]
        + [outside] * (len(inputs) + len(kept)),
        out_specs=[outside] * n_messages,
        input_output_aliases={1 + len(inputs) + n: n for n in range(len(kept))},
        scratch_shapes=[
            pltpu.VMEM((len(sides), 2, 4 * half, items), jnp.bfloat16),
            pltpu.VMEM((n_results, 2, half, items), jnp.bfloat16),
            pltpu.VMEM((n_results, 4 * half, half), jnp.bfloat16),
            pltpu.SemaphoreType.DMA((2 * len(groups),)),
            pltpu.SemaphoreType.DMA((2 * n_results,)),
            pltpu.SemaphoreType.DMA((n_results,)),
        ],
        compiler_params=pltpu.CompilerParams(vmem_limit_bytes=limit * 1024 * 1024),
        cost_estimate=pl.CostEstimate(
            flops=half * half, bytes_accessed=half * items, transcendentals=0
        ),
    )(place, *inputs, *kept)


def on_device(embeddings, basis, cov_prior):
    feat, batch = lax.axis_index("feat"), lax.axis_index("batch")
    x, yl, c = feat // 4, feat // 2 % 2, feat % 2
    z, yh = batch // 2, batch % 2
    items, feats = embeddings.shape
    half = feats // 2
    items_total = items * lax.axis_size("batch")
    place = jnp.stack([(x - z) % 4, yh]).astype(jnp.int32)

    whole = embeddings.T.reshape(2, half, items)
    inner, outer = pick(whole, yh), pick(whole, 1 - yh)
    near, far, whole_c = together([(inner, NEAR), (outer, FAR), (whole, CORE)])
    right = jnp.stack([near, far])
    share = narrow(jnp.dot(embeddings, basis, preferred_element_type=jnp.float32))
    width = share.shape[1]
    share = share.reshape(16, items // 16, width)

    below_n, above_f = together([(near, X_STEP[1]), (far, X_STEP[3])], (share,))
    near1, far1 = together([(outer, NEAR), (inner, FAR)], (near, far, share))
    below_f, above_n = together([(far, X_STEP[1]), (near, X_STEP[3])], (below_n, above_f))
    two0, two1, right_c = together(
        [(far, NEAR), (near, FAR), (right, CORE)], (near1, far1)
    )
    rim = jnp.stack([near1, far1])
    across = together([(below_n, X_STEP[1]), (above_f, X_STEP[3])], (below_f, above_n))
    (rim_c,) = together([(rim, CORE)])
    two0_c, two1_c = together([(two0, CORE), (two1, CORE)])
    side = (
        ((whole, "0"), two0),
        ((whole, "1"), two1),
        (near, far),
        (near1, far1),
    )
    side_c = (
        ((whole_c, "0"), two0_c),
        ((whole_c, "1"), two1_c),
        ((right_c, 0), (right_c, 1)),
        ((rim_c, 0), (rim_c, 1)),
    )
    early = {0: (near, far), 1: (above_n, above_f), 3: (below_n, below_f)}
    every = {0: (near, far), 1: (above_n, above_f), 2: tuple(across), 3: (below_n, below_f)}
    kept = block_product(place, {0: (side, (("dx", 0), ("dx", 1), ("dx", 3)))}, early)
    home_a, home_b, up, down_a, down_b, middle = block_product(
        place, {1: (side_c, (("dz", 2), ("dz", 3))), 0: (side, (("dx", 2),))}, every, kept
    )
    home_b, middle = block_product(
        place, {1: (side_c, (("dz", 1), ("dz", 0)))}, every, (home_b, middle), LATE
    )

    share, down_a, down_b, up = lax.optimization_barrier((share, down_a, down_b, up))
    shares = lax.all_to_all(share, "feat", 0, 0)
    down_a, up, down_b = together(
        [(down_a, Z_STEP[3]), (up, Z_STEP[1]), (down_b, Z_CROSS[3])]
    )
    (home_b,) = together([(home_b, CORE)])
    first, second = together(
        [
            (narrow(wide(down_a) + wide(middle[0])), Z_STEP[3]),
            (narrow(wide(up[1]) + wide(middle[1])), Z_CROSS[1]),
        ]
    )
    total = jnp.stack(
        [
            narrow(wide(home_a) + wide(up[0]) + wide(first)).reshape(2, 2 * half, half),
            narrow(wide(home_b) + wide(down_b) + wide(second)).reshape(2, 2 * half, half),
        ],
        1,
    )
    homeward = [pick(total, yl ^ yh ^ s) for s in range(2)]
    shares, homeward = lax.optimization_barrier((shares, homeward))
    projected = narrow(jnp.sum(wide(shares), 0))
    arrived = [send(v, HOME[s]) for s, v in enumerate(homeward)]
    *arrived, projected = lax.optimization_barrier((*arrived, projected))

    def quarter(q):
        t, s = q // 2, q % 2
        value = jnp.where(
            c == 0,
            jnp.where(yl == 0, arrived[s][t], arrived[1 - s][t]),
            jnp.where(yl == 0, arrived[s][1 - t], arrived[1 - s][1 - t]),
        )
        return jnp.concatenate([value[half:], value[:half]], 0) if s else value

    gram = jnp.concatenate([quarter(q) for q in range(4)], 1)
    covariance = 0.9 * cov_prior + wide(gram) / items_total
    return (covariance, projected)


def solution(mesh):
    placed = (P("batch", "feat"), P("feat", None), P("feat", "batch"))
    return jax.shard_map(
        on_device,
        mesh=mesh,
        in_specs=placed,
        out_specs=(P("feat", "batch"), P(("batch", "feat"), None)),
        check_vma=False,
    )
```

```python
import functools

import jax
import jax.numpy as jnp
from jax import lax
from jax.experimental import pallas as pl
from jax.experimental.pallas import tpu as pltpu
from jax.sharding import PartitionSpec as P

SIZES = (4, 2, 2, 4, 2)
AXES = ("feat", "batch")
LATE = 30


def flat(place):
    index = 0
    for value, size in zip(place, SIZES):
        index = index * size + value % size
    return index


def table(move):
    pairs = []
    for x in range(4):
        for yl in range(2):
            for c in range(2):
                for z in range(4):
                    for yh in range(2):
                        pairs.append((flat((x, yl, c, z, yh)), flat(move(x, yl, c, z, yh))))
    return pairs


CORE = table(lambda x, yl, c, z, yh: (x, yl, 1 - c, z, yh))
NEAR = table(lambda x, yl, c, z, yh: (x, 1 - yl, c, z, yh))
FAR = table(lambda x, yl, c, z, yh: (x, 1 - yl, c, z, 1 - yh))
X_STEP = {d: table(lambda x, yl, c, z, yh, d=d: (x + d, yl, c, z, yh)) for d in (1, 2, 3)}
Z_STEP = {d: table(lambda x, yl, c, z, yh, d=d: (x, yl, c, z + d, yh)) for d in (1, 3)}
HOME = {
    (s, t): table(lambda x, yl, c, z, yh, s=s, t=t: (x, yh ^ s, c ^ t, z, 1 - yl))
    for s in range(2)
    for t in range(2)
}


def send(value, pairs):
    return lax.ppermute(value, AXES, pairs)


def pick(array, index):
    return lax.dynamic_index_in_dim(array, index, 0, keepdims=False)


def wide(value):
    return value.astype(jnp.float32)


def narrow(value):
    return value.astype(jnp.bfloat16)


def together(sends, after=()):
    values, _ = lax.optimization_barrier(([value for value, _ in sends], after))
    results = [send(value, pairs) for value, (_, pairs) in zip(values, sends)]
    return lax.optimization_barrier(results)


def block_kernel(plan, sides, *refs):
    place, refs = refs[0], refs[1:]
    n_in = plan["inputs"]
    inputs, refs = refs[:n_in], refs[n_in + plan["kept"] :]
    if plan["messages"] == 4:
        home, up, down, middle = refs[:4]
    else:
        (home, middle), up, down = refs[:2], None, None
    targets = ((home, up, down, middle), (home, middle, up, down))
    refs = refs[plan["messages"] :]
    left, columns_in, result, left_sem, column_sem, out_sem = refs
    shift, high = place[0], place[1]
    rows = columns_in.shape[2]

    def view(name):
        index, part = name
        if part is None:
            return inputs[index]
        return inputs[index].at[part if isinstance(part, int) else (high ^ int(part))]

    jobs = [
        (side, cc, kind, which)
        for side, (cc, wanted) in enumerate(plan["sides"])
        for kind, which in wanted
    ]
    rights = []
    for slot, (_, _, kind, which) in enumerate(jobs):
        if kind == "dx":
            options = [(None, which)]
        else:
            dx = (which + 4 - shift) % 4
            options = [(dx == k, k) for k in plan["order"]]
        rights.append(
            [
                (
                    here,
                    pltpu.make_async_copy(
                        view(plan["blocks"][plan["order"].index(k)][i]),
                        columns_in.at[slot, i],
                        column_sem.at[2 * slot + i],
                    ),
                )
                for here, k in options
                for i in range(2)
            ]
        )
    lefts = [
        pltpu.make_async_copy(
            view(name),
            left.at[k // 4, i, pl.ds(k % 4 * rows, rows)],
            left_sem.at[2 * k + i],
        )
        for k, names in enumerate(sides)
        for i, name in enumerate(names)
    ]

    def each(copies, act):
        for here, copy in copies:
            if here is None:
                getattr(copy, act)()
            else:
                pl.when(here)(getattr(copy, act))

    for slot, (side, *_) in enumerate(jobs):
        each(rights[slot], "start")
        if slot == 0 or jobs[slot - 1][0] != side:
            each([(None, copy) for copy in lefts[8 * side : 8 * side + 8]], "start")
    outs = []
    for side, (cc, wanted) in enumerate(plan["sides"]):
        slots = [slot for slot, job in enumerate(jobs) if job[0] == side]
        each([(None, copy) for copy in lefts[8 * side : 8 * side + 8]], "wait")
        for slot in slots:
            each(rights[slot], "wait")

        def multiply(slot, carry):
            for group in range(4):
                here = slice(group * rows, (group + 1) * rows)
                total = None
                for i in range(2):
                    term = lax.dot_general(
                        left[side, i, here],
                        columns_in[slot, i],
                        (((1,), (1,)), ((), ())),
                        preferred_element_type=jnp.float32,
                    )
                    total = term if total is None else total + term
                result[slot, here] = total.astype(jnp.bfloat16)
            return carry

        lax.fori_loop(slots[0], slots[-1] + 1, multiply, 0)
        for slot, (kind, which) in zip(slots, wanted):
            dz = (shift + which) % 4
            options = [(dz == d, d) for d in range(4)] if kind == "dx" else [(None, which)]
            copies = [
                (
                    here,
                    pltpu.make_async_copy(
                        result.at[slot], targets[cc][d].at[cc], out_sem.at[slot]
                    ),
                )
                for here, d in options
            ]
            each(copies, "start")
            outs += copies
    each(outs, "wait")


def block_product(place, sides, blocks, kept=(), limit=60):
    inputs = []

    def enter(piece):
        array, part = piece if isinstance(piece, tuple) else (piece, None)
        for index, known in enumerate(inputs):
            if known is array:
                return index, part
        inputs.append(array)
        return len(inputs) - 1, part

    groups = [[enter(piece) for piece in pair] for side, _ in sides.values() for pair in side]
    names = [[enter(piece) for piece in pair] for pair in blocks.values()]
    half, items = inputs[0].shape[-2:]
    wanted = tuple((cc, jobs) for cc, (_, jobs) in sides.items())
    n_results = sum(len(jobs) for _, jobs in wanted)
    n_messages = len(kept) or 4
    plan = {
        "inputs": len(inputs),
        "kept": len(kept),
        "messages": n_messages,
        "sides": wanted,
        "blocks": names,
        "order": tuple(blocks),
    }
    outside = pl.BlockSpec(memory_space=pltpu.HBM)
    n_blocks = len(blocks)
    return pl.pallas_call(
        functools.partial(block_kernel, plan, groups),
        out_shape=[jax.ShapeDtypeStruct((2, 4 * half, half), jnp.bfloat16)] * n_messages,
        in_specs=[pl.BlockSpec(memory_space=pltpu.SMEM)]
        + [outside] * (len(inputs) + len(kept)),
        out_specs=[outside] * n_messages,
        input_output_aliases={1 + len(inputs) + n: n for n in range(len(kept))},
        scratch_shapes=[
            pltpu.VMEM((len(sides), 2, 4 * half, items), jnp.bfloat16),
            pltpu.VMEM((n_results, 2, half, items), jnp.bfloat16),
            pltpu.VMEM((n_results, 4 * half, half), jnp.bfloat16),
            pltpu.SemaphoreType.DMA((2 * len(groups),)),
            pltpu.SemaphoreType.DMA((2 * n_results,)),
            pltpu.SemaphoreType.DMA((n_results,)),
        ],
        compiler_params=pltpu.CompilerParams(vmem_limit_bytes=limit * 1024 * 1024),
        cost_estimate=pl.CostEstimate(
            flops=half * half, bytes_accessed=half * items, transcendentals=0
        ),
    )(place, *inputs, *kept)


def on_device(embeddings, basis, cov_prior):
    feat, batch = lax.axis_index("feat"), lax.axis_index("batch")
    x, yl, c = feat // 4, feat // 2 % 2, feat % 2
    z, yh = batch // 2, batch % 2
    items, feats = embeddings.shape
    half = feats // 2
    items_total = items * lax.axis_size("batch")
    place = jnp.stack([(x - z) % 4, yh]).astype(jnp.int32)

    whole = embeddings.T.reshape(2, half, items)
    inner, outer = pick(whole, yh), pick(whole, 1 - yh)
    near, far, whole_c = together([(inner, NEAR), (outer, FAR), (whole, CORE)])
    right = jnp.stack([near, far])
    share = narrow(jnp.dot(embeddings, basis, preferred_element_type=jnp.float32))
    width = share.shape[1]
    share = share.reshape(16, items // 16, width)

    below_n, above_f = together([(near, X_STEP[1]), (far, X_STEP[3])], (share,))
    near1, far1 = together([(outer, NEAR), (inner, FAR)], (near, far, share))
    below_f, above_n = together([(far, X_STEP[1]), (near, X_STEP[3])], (below_n, above_f))
    two0, two1, right_c = together(
        [(far, NEAR), (near, FAR), (right, CORE)], (near1, far1)
    )
    rim = jnp.stack([near1, far1])
    across = together([(below_n, X_STEP[1]), (above_f, X_STEP[3])], (below_f, above_n))
    (rim_c,) = together([(rim, CORE)])
    two0_c, two1_c = together([(two0, CORE), (two1, CORE)])
    side = (
        ((whole, "0"), two0),
        ((whole, "1"), two1),
        (near, far),
        (near1, far1),
    )
    side_c = (
        ((whole_c, "0"), two0_c),
        ((whole_c, "1"), two1_c),
        ((right_c, 0), (right_c, 1)),
        ((rim_c, 0), (rim_c, 1)),
    )
    early = {0: (near, far), 1: (above_n, above_f), 3: (below_n, below_f)}
    every = {0: (near, far), 1: (above_n, above_f), 2: tuple(across), 3: (below_n, below_f)}
    kept = block_product(place, {0: (side, (("dx", 0), ("dx", 1), ("dx", 3)))}, early)
    home, up, down, middle = block_product(
        place, {1: (side_c, (("dz", 2), ("dz", 3))), 0: (side, (("dx", 2),))}, every, kept
    )
    home, middle = block_product(
        place, {1: (side_c, (("dz", 1), ("dz", 0)))}, every, (home, middle), LATE
    )

    share, down, up = lax.optimization_barrier((share, down, up))
    shares = lax.all_to_all(share, "feat", 0, 0)
    down, up = together([(down, Z_STEP[3]), (up, Z_STEP[1])])
    first, second = together(
        [
            (narrow(wide(down[0]) + wide(middle[0])), Z_STEP[3]),
            (narrow(wide(up[1]) + wide(middle[1])), Z_STEP[1]),
        ]
    )
    total = [
        narrow(wide(home[0]) + wide(up[0]) + wide(first)).reshape(2, 2 * half, half),
        narrow(wide(home[1]) + wide(down[1]) + wide(second)).reshape(2, 2 * half, half),
    ]
    homeward = [pick(total[t], yl ^ yh ^ s) for s in range(2) for t in range(2)]
    shares, homeward = lax.optimization_barrier((shares, homeward))
    projected = narrow(jnp.sum(wide(shares), 0))
    arrived = [send(v, HOME[s // 2, s % 2]) for s, v in enumerate(homeward)]
    *arrived, projected = lax.optimization_barrier((*arrived, projected))

    def quarter(q):
        t, s = q // 2, q % 2
        value = jnp.where(
            c == 0,
            jnp.where(yl == 0, arrived[2 * s + t], arrived[2 - 2 * s + t]),
            jnp.where(yl == 0, arrived[2 * s + 1 - t], arrived[3 - 2 * s - t]),
        )
        return jnp.concatenate([value[half:], value[:half]], 0) if s else value

    gram = jnp.concatenate([quarter(q) for q in range(4)], 1)
    covariance = 0.9 * cov_prior + wide(gram) / items_total
    return (covariance, projected)


def solution(mesh):
    placed = (P("batch", "feat"), P("feat", None), P("feat", "batch"))
    return jax.shard_map(
        on_device,
        mesh=mesh,
        in_specs=placed,
        out_specs=(P("feat", "batch"), P(("batch", "feat"), None)),
        check_vma=False,
    )
```

```python
import functools

import jax
import jax.numpy as jnp
from jax import lax
from jax.experimental import pallas as pl
from jax.experimental.pallas import tpu as pltpu
from jax.sharding import PartitionSpec as P

SIZES = (4, 2, 2, 4, 2)
AXES = ("feat", "batch")
LATE = 60


def flat(place):
    index = 0
    for value, size in zip(place, SIZES):
        index = index * size + value % size
    return index


def table(move):
    pairs = []
    for x in range(4):
        for yl in range(2):
            for c in range(2):
                for z in range(4):
                    for yh in range(2):
                        pairs.append((flat((x, yl, c, z, yh)), flat(move(x, yl, c, z, yh))))
    return pairs


CORE = table(lambda x, yl, c, z, yh: (x, yl, 1 - c, z, yh))
NEAR = table(lambda x, yl, c, z, yh: (x, 1 - yl, c, z, yh))
FAR = table(lambda x, yl, c, z, yh: (x, 1 - yl, c, z, 1 - yh))
X_STEP = {d: table(lambda x, yl, c, z, yh, d=d: (x + d, yl, c, z, yh)) for d in (1, 2, 3)}
Z_STEP = {d: table(lambda x, yl, c, z, yh, d=d: (x, yl, c, z + d, yh)) for d in (1, 3)}
HOME = {
    (s, t): table(lambda x, yl, c, z, yh, s=s, t=t: (x, yh ^ s, c ^ t, z, 1 - yl))
    for s in range(2)
    for t in range(2)
}


def send(value, pairs):
    return lax.ppermute(value, AXES, pairs)


def pick(array, index):
    return lax.dynamic_index_in_dim(array, index, 0, keepdims=False)


def wide(value):
    return value.astype(jnp.float32)


def narrow(value):
    return value.astype(jnp.bfloat16)


def together(sends, after=()):
    values, _ = lax.optimization_barrier(([value for value, _ in sends], after))
    results = [send(value, pairs) for value, (_, pairs) in zip(values, sends)]
    return lax.optimization_barrier(results)


def block_kernel(plan, sides, *refs):
    place, refs = refs[0], refs[1:]
    n_in = plan["inputs"]
    inputs, refs = refs[:n_in], refs[n_in + plan["kept"] :]
    if plan["messages"] == 4:
        home, up, down, middle = refs[:4]
    else:
        (home, middle), up, down = refs[:2], None, None
    targets = ((home, up, down, middle), (home, middle, up, down))
    refs = refs[plan["messages"] :]
    left, columns_in, result, left_sem, column_sem, out_sem = refs
    shift, high = place[0], place[1]
    rows = columns_in.shape[2]

    def view(name):
        index, part = name
        if part is None:
            return inputs[index]
        return inputs[index].at[part if isinstance(part, int) else (high ^ int(part))]

    jobs = [
        (side, cc, kind, which)
        for side, (cc, wanted) in enumerate(plan["sides"])
        for kind, which in wanted
    ]
    rights = []
    for slot, (_, _, kind, which) in enumerate(jobs):
        if kind == "dx":
            options = [(None, which)]
        else:
            dx = (which + 4 - shift) % 4
            options = [(dx == k, k) for k in plan["order"]]
        rights.append(
            [
                (
                    here,
                    pltpu.make_async_copy(
                        view(plan["blocks"][plan["order"].index(k)][i]),
                        columns_in.at[slot, i],
                        column_sem.at[2 * slot + i],
                    ),
                )
                for here, k in options
                for i in range(2)
            ]
        )
    lefts = [
        pltpu.make_async_copy(
            view(name),
            left.at[k // 4, i, pl.ds(k % 4 * rows, rows)],
            left_sem.at[2 * k + i],
        )
        for k, names in enumerate(sides)
        for i, name in enumerate(names)
    ]

    def each(copies, act):
        for here, copy in copies:
            if here is None:
                getattr(copy, act)()
            else:
                pl.when(here)(getattr(copy, act))

    for slot, (side, *_) in enumerate(jobs):
        each(rights[slot], "start")
        if slot == 0 or jobs[slot - 1][0] != side:
            each([(None, copy) for copy in lefts[8 * side : 8 * side + 8]], "start")
    outs = []
    for side, (cc, wanted) in enumerate(plan["sides"]):
        slots = [slot for slot, job in enumerate(jobs) if job[0] == side]
        each([(None, copy) for copy in lefts[8 * side : 8 * side + 8]], "wait")
        for slot in slots:
            each(rights[slot], "wait")

        def multiply(slot, carry):
            for group in range(4):
                here = slice(group * rows, (group + 1) * rows)
                total = None
                for i in range(2):
                    term = lax.dot_general(
                        left[side, i, here],
                        columns_in[slot, i],
                        (((1,), (1,)), ((), ())),
                        preferred_element_type=jnp.float32,
                    )
                    total = term if total is None else total + term
                result[slot, here] = total.astype(jnp.bfloat16)
            return carry

        lax.fori_loop(slots[0], slots[-1] + 1, multiply, 0)
        for slot, (kind, which) in zip(slots, wanted):
            dz = (shift + which) % 4
            options = [(dz == d, d) for d in range(4)] if kind == "dx" else [(None, which)]
            copies = [
                (
                    here,
                    pltpu.make_async_copy(
                        result.at[slot], targets[cc][d].at[cc], out_sem.at[slot]
                    ),
                )
                for here, d in options
            ]
            each(copies, "start")
            outs += copies
    each(outs, "wait")


def block_product(place, sides, blocks, kept=(), limit=60):
    inputs = []

    def enter(piece):
        array, part = piece if isinstance(piece, tuple) else (piece, None)
        for index, known in enumerate(inputs):
            if known is array:
                return index, part
        inputs.append(array)
        return len(inputs) - 1, part

    groups = [[enter(piece) for piece in pair] for side, _ in sides.values() for pair in side]
    names = [[enter(piece) for piece in pair] for pair in blocks.values()]
    half, items = inputs[0].shape[-2:]
    wanted = tuple((cc, jobs) for cc, (_, jobs) in sides.items())
    n_results = sum(len(jobs) for _, jobs in wanted)
    n_messages = len(kept) or 4
    plan = {
        "inputs": len(inputs),
        "kept": len(kept),
        "messages": n_messages,
        "sides": wanted,
        "blocks": names,
        "order": tuple(blocks),
    }
    outside = pl.BlockSpec(memory_space=pltpu.HBM)
    n_blocks = len(blocks)
    return pl.pallas_call(
        functools.partial(block_kernel, plan, groups),
        out_shape=[jax.ShapeDtypeStruct((2, 4 * half, half), jnp.bfloat16)] * n_messages,
        in_specs=[pl.BlockSpec(memory_space=pltpu.SMEM)]
        + [outside] * (len(inputs) + len(kept)),
        out_specs=[outside] * n_messages,
        input_output_aliases={1 + len(inputs) + n: n for n in range(len(kept))},
        scratch_shapes=[
            pltpu.VMEM((len(sides), 2, 4 * half, items), jnp.bfloat16),
            pltpu.VMEM((n_results, 2, half, items), jnp.bfloat16),
            pltpu.VMEM((n_results, 4 * half, half), jnp.bfloat16),
            pltpu.SemaphoreType.DMA((2 * len(groups),)),
            pltpu.SemaphoreType.DMA((2 * n_results,)),
            pltpu.SemaphoreType.DMA((n_results,)),
        ],
        compiler_params=pltpu.CompilerParams(vmem_limit_bytes=limit * 1024 * 1024),
        cost_estimate=pl.CostEstimate(
            flops=half * half, bytes_accessed=half * items, transcendentals=0
        ),
    )(place, *inputs, *kept)


def on_device(embeddings, basis, cov_prior):
    feat, batch = lax.axis_index("feat"), lax.axis_index("batch")
    x, yl, c = feat // 4, feat // 2 % 2, feat % 2
    z, yh = batch // 2, batch % 2
    items, feats = embeddings.shape
    half = feats // 2
    items_total = items * lax.axis_size("batch")
    place = jnp.stack([(x - z) % 4, yh]).astype(jnp.int32)

    whole = embeddings.T.reshape(2, half, items)
    inner, outer = pick(whole, yh), pick(whole, 1 - yh)
    near, far, whole_c = together([(inner, NEAR), (outer, FAR), (whole, CORE)])
    right = jnp.stack([near, far])
    share = narrow(jnp.dot(embeddings, basis, preferred_element_type=jnp.float32))
    width = share.shape[1]
    share = share.reshape(16, items // 16, width)

    below_n, above_f = together([(near, X_STEP[1]), (far, X_STEP[3])], (share,))
    near1, far1 = together([(outer, NEAR), (inner, FAR)], (near, far, share))
    below_f, above_n = together([(far, X_STEP[1]), (near, X_STEP[3])], (below_n, above_f))
    two0, two1, right_c = together(
        [(far, NEAR), (near, FAR), (right, CORE)], (near1, far1)
    )
    rim = jnp.stack([near1, far1])
    across = together([(below_n, X_STEP[1]), (above_f, X_STEP[3])], (below_f, above_n))
    (rim_c,) = together([(rim, CORE)])
    two0_c, two1_c = together([(two0, CORE), (two1, CORE)])
    side = (
        ((whole, "0"), two0),
        ((whole, "1"), two1),
        (near, far),
        (near1, far1),
    )
    side_c = (
        ((whole_c, "0"), two0_c),
        ((whole_c, "1"), two1_c),
        ((right_c, 0), (right_c, 1)),
        ((rim_c, 0), (rim_c, 1)),
    )
    early = {0: (near, far), 1: (above_n, above_f), 3: (below_n, below_f)}
    every = {0: (near, far), 1: (above_n, above_f), 2: tuple(across), 3: (below_n, below_f)}
    kept = block_product(place, {0: (side, (("dx", 0), ("dx", 1), ("dx", 3)))}, early)
    home, up, down, middle = block_product(
        place, {1: (side_c, (("dz", 2), ("dz", 3))), 0: (side, (("dx", 2),))}, every, kept
    )
    home, middle = block_product(
        place, {1: (side_c, (("dz", 1), ("dz", 0)))}, every, (home, middle), LATE
    )

    share, down, up = lax.optimization_barrier((share, down, up))
    shares = lax.all_to_all(share, "feat", 0, 0)
    down, up = together([(down, Z_STEP[3]), (up, Z_STEP[1])])
    first, second = together(
        [
            (narrow(wide(down[0]) + wide(middle[0])), Z_STEP[3]),
            (narrow(wide(up[1]) + wide(middle[1])), Z_STEP[1]),
        ]
    )
    total = [
        narrow(wide(home[0]) + wide(up[0]) + wide(first)).reshape(2, 2 * half, half),
        narrow(wide(home[1]) + wide(down[1]) + wide(second)).reshape(2, 2 * half, half),
    ]
    homeward = [pick(total[t], yl ^ yh ^ s) for s in range(2) for t in range(2)]
    shares, homeward = lax.optimization_barrier((shares, homeward))
    projected = narrow(jnp.sum(wide(shares), 0))
    sent = [send(homeward[n], HOME[n // 2, n % 2]) for n in (2, 0, 3, 1)]
    *sent, projected = lax.optimization_barrier((*sent, projected))
    arrived = [sent[n] for n in (1, 3, 0, 2)]

    def quarter(q):
        t, s = q // 2, q % 2
        value = jnp.where(
            c == 0,
            jnp.where(yl == 0, arrived[2 * s + t], arrived[2 - 2 * s + t]),
            jnp.where(yl == 0, arrived[2 * s + 1 - t], arrived[3 - 2 * s - t]),
        )
        return jnp.concatenate([value[half:], value[:half]], 0) if s else value

    gram = jnp.concatenate([quarter(q) for q in range(4)], 1)
    covariance = 0.9 * cov_prior + wide(gram) / items_total
    return (covariance, projected)


def solution(mesh):
    placed = (P("batch", "feat"), P("feat", None), P("feat", "batch"))
    return jax.shard_map(
        on_device,
        mesh=mesh,
        in_specs=placed,
        out_specs=(P("feat", "batch"), P(("batch", "feat"), None)),
        check_vma=False,
    )
```

```python
import functools

import jax
import jax.numpy as jnp
from jax import lax
from jax.experimental import pallas as pl
from jax.experimental.pallas import tpu as pltpu
from jax.sharding import PartitionSpec as P

SIZES = (4, 2, 2, 4, 2)
AXES = ("feat", "batch")
LATE = 60


def flat(place):
    index = 0
    for value, size in zip(place, SIZES):
        index = index * size + value % size
    return index


def table(move):
    pairs = []
    for x in range(4):
        for yl in range(2):
            for c in range(2):
                for z in range(4):
                    for yh in range(2):
                        pairs.append((flat((x, yl, c, z, yh)), flat(move(x, yl, c, z, yh))))
    return pairs


CORE = table(lambda x, yl, c, z, yh: (x, yl, 1 - c, z, yh))
NEAR = table(lambda x, yl, c, z, yh: (x, 1 - yl, c, z, yh))
FAR = table(lambda x, yl, c, z, yh: (x, 1 - yl, c, z, 1 - yh))
X_STEP = {d: table(lambda x, yl, c, z, yh, d=d: (x + d, yl, c, z, yh)) for d in (1, 2, 3)}
Z_STEP = {d: table(lambda x, yl, c, z, yh, d=d: (x, yl, c, z + d, yh)) for d in (1, 3)}
HOME = {
    (s, t): table(lambda x, yl, c, z, yh, s=s, t=t: (x, yh ^ s, c ^ t, z, 1 - yl))
    for s in range(2)
    for t in range(2)
}


def send(value, pairs):
    return lax.ppermute(value, AXES, pairs)


def pick(array, index):
    return lax.dynamic_index_in_dim(array, index, 0, keepdims=False)


def wide(value):
    return value.astype(jnp.float32)


def narrow(value):
    return value.astype(jnp.bfloat16)


def together(sends, after=()):
    values, _ = lax.optimization_barrier(([value for value, _ in sends], after))
    results = [send(value, pairs) for value, (_, pairs) in zip(values, sends)]
    return lax.optimization_barrier(results)


def block_kernel(plan, sides, *refs):
    place, refs = refs[0], refs[1:]
    n_in = plan["inputs"]
    inputs, refs = refs[:n_in], refs[n_in + plan["kept"] :]
    if plan["messages"] == 4:
        home, up, down, middle = refs[:4]
    else:
        (home, middle), up, down = refs[:2], None, None
    targets = ((home, up, down, middle), (home, middle, up, down))
    refs = refs[plan["messages"] :]
    left, columns_in, result, left_sem, column_sem, out_sem = refs
    shift, high = place[0], place[1]
    rows = columns_in.shape[2]

    def view(name):
        index, part = name
        if part is None:
            return inputs[index]
        return inputs[index].at[part if isinstance(part, int) else (high ^ int(part))]

    jobs = [
        (side, cc, kind, which)
        for side, (cc, wanted) in enumerate(plan["sides"])
        for kind, which in wanted
    ]
    rights = []
    for slot, (_, _, kind, which) in enumerate(jobs):
        if kind == "dx":
            options = [(None, which)]
        else:
            dx = (which + 4 - shift) % 4
            options = [(dx == k, k) for k in plan["order"]]
        rights.append(
            [
                (
                    here,
                    pltpu.make_async_copy(
                        view(plan["blocks"][plan["order"].index(k)][i]),
                        columns_in.at[slot, i],
                        column_sem.at[2 * slot + i],
                    ),
                )
                for here, k in options
                for i in range(2)
            ]
        )
    lefts = [
        pltpu.make_async_copy(
            view(name),
            left.at[k // 4, i, pl.ds(k % 4 * rows, rows)],
            left_sem.at[2 * k + i],
        )
        for k, names in enumerate(sides)
        for i, name in enumerate(names)
    ]

    def each(copies, act):
        for here, copy in copies:
            if here is None:
                getattr(copy, act)()
            else:
                pl.when(here)(getattr(copy, act))

    for slot, (side, *_) in enumerate(jobs):
        each(rights[slot], "start")
        if slot == 0 or jobs[slot - 1][0] != side:
            each([(None, copy) for copy in lefts[8 * side : 8 * side + 8]], "start")
    outs = []
    for side, (cc, wanted) in enumerate(plan["sides"]):
        slots = [slot for slot, job in enumerate(jobs) if job[0] == side]
        each([(None, copy) for copy in lefts[8 * side : 8 * side + 8]], "wait")
        for slot in slots:
            each(rights[slot], "wait")

        def multiply(slot, carry):
            for group in range(4):
                here = slice(group * rows, (group + 1) * rows)
                total = None
                for i in range(2):
                    term = lax.dot_general(
                        left[side, i, here],
                        columns_in[slot, i],
                        (((1,), (1,)), ((), ())),
                        preferred_element_type=jnp.float32,
                    )
                    total = term if total is None else total + term
                result[slot, here] = total.astype(jnp.bfloat16)
            return carry

        lax.fori_loop(slots[0], slots[-1] + 1, multiply, 0)
        for slot, (kind, which) in zip(slots, wanted):
            dz = (shift + which) % 4
            options = [(dz == d, d) for d in range(4)] if kind == "dx" else [(None, which)]
            copies = [
                (
                    here,
                    pltpu.make_async_copy(
                        result.at[slot], targets[cc][d].at[cc], out_sem.at[slot]
                    ),
                )
                for here, d in options
            ]
            each(copies, "start")
            outs += copies
    each(outs, "wait")


def block_product(place, sides, blocks, kept=(), limit=60):
    inputs = []

    def enter(piece):
        array, part = piece if isinstance(piece, tuple) else (piece, None)
        for index, known in enumerate(inputs):
            if known is array:
                return index, part
        inputs.append(array)
        return len(inputs) - 1, part

    groups = [[enter(piece) for piece in pair] for side, _ in sides.values() for pair in side]
    names = [[enter(piece) for piece in pair] for pair in blocks.values()]
    half, items = inputs[0].shape[-2:]
    wanted = tuple((cc, jobs) for cc, (_, jobs) in sides.items())
    n_results = sum(len(jobs) for _, jobs in wanted)
    n_messages = len(kept) or 4
    plan = {
        "inputs": len(inputs),
        "kept": len(kept),
        "messages": n_messages,
        "sides": wanted,
        "blocks": names,
        "order": tuple(blocks),
    }
    outside = pl.BlockSpec(memory_space=pltpu.HBM)
    n_blocks = len(blocks)
    return pl.pallas_call(
        functools.partial(block_kernel, plan, groups),
        out_shape=[jax.ShapeDtypeStruct((2, 4 * half, half), jnp.bfloat16)] * n_messages,
        in_specs=[pl.BlockSpec(memory_space=pltpu.SMEM)]
        + [outside] * (len(inputs) + len(kept)),
        out_specs=[outside] * n_messages,
        input_output_aliases={1 + len(inputs) + n: n for n in range(len(kept))},
        scratch_shapes=[
            pltpu.VMEM((len(sides), 2, 4 * half, items), jnp.bfloat16),
            pltpu.VMEM((n_results, 2, half, items), jnp.bfloat16),
            pltpu.VMEM((n_results, 4 * half, half), jnp.bfloat16),
            pltpu.SemaphoreType.DMA((2 * len(groups),)),
            pltpu.SemaphoreType.DMA((2 * n_results,)),
            pltpu.SemaphoreType.DMA((n_results,)),
        ],
        compiler_params=pltpu.CompilerParams(vmem_limit_bytes=limit * 1024 * 1024),
        cost_estimate=pl.CostEstimate(
            flops=half * half, bytes_accessed=half * items, transcendentals=0
        ),
    )(place, *inputs, *kept)


def on_device(embeddings, basis, cov_prior):
    feat, batch = lax.axis_index("feat"), lax.axis_index("batch")
    x, yl, c = feat // 4, feat // 2 % 2, feat % 2
    z, yh = batch // 2, batch % 2
    items, feats = embeddings.shape
    half = feats // 2
    items_total = items * lax.axis_size("batch")
    place = jnp.stack([(x - z) % 4, yh]).astype(jnp.int32)

    whole = embeddings.T.reshape(2, half, items)
    inner, outer = pick(whole, yh), pick(whole, 1 - yh)
    near, far, whole_c = together([(inner, NEAR), (outer, FAR), (whole, CORE)])
    right = jnp.stack([near, far])
    share = narrow(jnp.dot(embeddings, basis, preferred_element_type=jnp.float32))
    width = share.shape[1]
    share = share.reshape(16, items // 16, width)

    below_n, above_f = together([(near, X_STEP[1]), (far, X_STEP[3])], (share,))
    near1, far1 = together([(outer, NEAR), (inner, FAR)], (near, far, share))
    below_f, above_n = together([(far, X_STEP[1]), (near, X_STEP[3])], (below_n, above_f))
    two0, two1, right_c = together(
        [(far, NEAR), (near, FAR), (right, CORE)], (near1, far1)
    )
    rim = jnp.stack([near1, far1])
    across = together([(below_n, X_STEP[1]), (above_f, X_STEP[3])], (below_f, above_n))
    (rim_c,) = together([(rim, CORE)])
    two0_c, two1_c = together([(two0, CORE), (two1, CORE)])
    side = (
        ((whole, "0"), two0),
        ((whole, "1"), two1),
        (near, far),
        (near1, far1),
    )
    side_c = (
        ((whole_c, "0"), two0_c),
        ((whole_c, "1"), two1_c),
        ((right_c, 0), (right_c, 1)),
        ((rim_c, 0), (rim_c, 1)),
    )
    early = {0: (near, far), 1: (above_n, above_f), 3: (below_n, below_f)}
    every = {0: (near, far), 1: (above_n, above_f), 2: tuple(across), 3: (below_n, below_f)}
    kept = block_product(place, {0: (side, (("dx", 0), ("dx", 1), ("dx", 3)))}, early)
    home, up, down, middle = block_product(
        place, {1: (side_c, (("dz", 2), ("dz", 3))), 0: (side, (("dx", 2),))}, every, kept
    )
    home, middle = block_product(
        place, {1: (side_c, (("dz", 1), ("dz", 0)))}, every, (home, middle), LATE
    )

    share, down, up = lax.optimization_barrier((share, down, up))
    shares = lax.all_to_all(share, "feat", 0, 0)
    down, up = together([(down, Z_STEP[3]), (up, Z_STEP[1])])
    first, second = together(
        [
            (narrow(wide(down[0]) + wide(middle[0])), Z_STEP[3]),
            (narrow(wide(up[1]) + wide(middle[1])), Z_STEP[1]),
        ]
    )
    total = [
        narrow(wide(home[0]) + wide(up[0]) + wide(first)).reshape(2, 2 * half, half),
        narrow(wide(home[1]) + wide(down[1]) + wide(second)).reshape(2, 2 * half, half),
    ]
    homeward = [pick(total[t], yl ^ yh ^ s) for s in range(2) for t in range(2)]
    shares, homeward = lax.optimization_barrier((shares, homeward))
    projected = narrow(jnp.sum(wide(shares), 0))
    sent = [send(homeward[n], HOME[n // 2, n % 2]) for n in (2, 3, 0, 1)]
    *sent, projected = lax.optimization_barrier((*sent, projected))
    arrived = [sent[n] for n in (2, 3, 0, 1)]

    def quarter(q):
        t, s = q // 2, q % 2
        value = jnp.where(
            c == 0,
            jnp.where(yl == 0, arrived[2 * s + t], arrived[2 - 2 * s + t]),
            jnp.where(yl == 0, arrived[2 * s + 1 - t], arrived[3 - 2 * s - t]),
        )
        return jnp.concatenate([value[half:], value[:half]], 0) if s else value

    gram = jnp.concatenate([quarter(q) for q in range(4)], 1)
    covariance = 0.9 * cov_prior + wide(gram) / items_total
    return (covariance, projected)


def solution(mesh):
    placed = (P("batch", "feat"), P("feat", None), P("feat", "batch"))
    return jax.shard_map(
        on_device,
        mesh=mesh,
        in_specs=placed,
        out_specs=(P("feat", "batch"), P(("batch", "feat"), None)),
        check_vma=False,
    )
```
